128 devices in a mesh: aux: 32 (over y, x, z_hi), pan: 4 (over z_lo, core).
Axes of the slice: x: 4, y: 4, z: 4 (z_hi: 2, z_lo: 2; z = z_hi * 2 + z_lo), core: 2. Of those that a mesh axis runs over, the one named last changes fastest.
Arguments:
- slabs: bfloat16 [8, 6144, 4096], P(None, ('aux', 'pan')), may hold values from -0.5 to 0.5
- occ_energy: int32 [8], replicated, may hold values from -3072 to -257
- vir_energy: int32 [4096], replicated, may hold values from 256 to 4095
- i_index: int32 [2], replicated, may hold values from 0 to 7
- j_index: int32 [2], replicated, may hold values from 0 to 7
Outputs:
- gamma: float32 [2, 6144, 4096], P(None, ('aux', 'pan'))
The draws below stay inside these ranges and needn't reach their ends.
Inputs may be any that keep to these rules, and one draw needn't show every extreme that they name: `i_index`: indices of held slabs; an i may equal a j. `j_index`: indices of held slabs.
All inputs are finite; a program needn't handle non-finite values.
Results may differ from the reference program's by a relative error of at most 0.0019.
Values may be sent and summed in bfloat16 or wider, within the bound.
A program may use at most 128 MiB of HBM per device.

```python
import jax
import jax.numpy as jnp
from jax import lax

NAUX = 6144
NVIR = 4096
OCC_WIN = 8
I_WIN = 2
J_WIN = 2


def touch_ends(values, own_key, low, high):
    longest = values.shape.index(max(values.shape))
    spots = []
    for shift in (0, 1):
        where = [jax.random.randint(jax.random.fold_in(own_key, axis), (), 0, length) for axis, length in enumerate(values.shape)]
        where[longest] = (where[longest] + shift) % values.shape[longest]
        spots.append(tuple(where))
    return values.at[spots[0]].set(low).at[spots[1]].set(high)


def steps_of(key, extent, shards, low, top_value):
    gain, own = 1.0, jax.random.fold_in(key, 6)
    for dim, shards_of in shards:
        draws = jnp.exp(jax.random.uniform(jax.random.fold_in(own, dim), (shards_of,), jnp.float32, low / len(shards), top_value / len(shards)))
        gain = gain * jnp.repeat(draws, extent[dim] // shards_of).reshape([-1 if axis == dim else 1 for axis in range(len(extent))])
    return gain


def bell_draw(rng, shape, width, bound, cuts=(), kind=jnp.bfloat16):
    array = jax.random.normal(rng, shape, jnp.float32) * width
    if len(cuts) > 0:
        array = steps_of(rng, shape, cuts, -0.22, 0.18) * array
    return jnp.clip(array, min=-bound, max=bound).astype(kind)


def setup_inputs(seed: int = 0) -> dict:
    seeds = jax.random.split(jax.random.key(seed), 6)
    slabs = bell_draw(seeds[0], (OCC_WIN, NAUX, NVIR), 0.08, 0.5, ((1, 128),))
    occ_energy = touch_ends(jax.random.randint(seeds[1], (OCC_WIN,), -3072, -256), jax.random.fold_in(seeds[1], 1), -3072, (-256) - 1).astype(jnp.int32)
    vir_energy = touch_ends(jax.random.randint(seeds[2], (NVIR,), 256, 4096), jax.random.fold_in(seeds[2], 1), 256, 4095).astype(jnp.int32)
    i_index = jax.random.randint(seeds[3], (I_WIN,), 0, OCC_WIN).astype(jnp.int32)
    j_index = jax.random.randint(seeds[4], (J_WIN,), 0, OCC_WIN).astype(jnp.int32)
    return {"slabs": slabs, "occ_energy": occ_energy, "vir_energy": vir_energy, "i_index": i_index, "j_index": j_index}


energy_unit = 1.0 / 1024.0


def reference(slabs, occ_energy, vir_energy, i_index, j_index):
    occupied = occ_energy.astype(jnp.float32)
    virtual = vir_energy.astype(jnp.float32)
    results = []
    for i_slot in range(I_WIN):
        left_slab = slabs[i_index[i_slot]]
        total = jnp.zeros((NAUX, NVIR), jnp.float32)
        for j_slot in range(J_WIN):
            right_slab = slabs[j_index[j_slot]]
            integrals = lax.dot_general(left_slab, right_slab, (((0,), (0,)), ((), ())), preferred_element_type=jnp.float32)
            denominator = (virtual[:, None] + virtual[None, :] - occupied[i_index[i_slot]] - occupied[j_index[j_slot]]) * energy_unit
            amplitude = (integrals / denominator).astype(jnp.bfloat16)
            total = total + lax.dot_general(right_slab, amplitude, (((1,), (1,)), ((), ())), preferred_element_type=jnp.float32)
        results.append(total)
    return jnp.stack(results)
```

```python
import jax
import jax.numpy as jnp
from jax import lax
from jax.experimental import pallas as pl
from jax.experimental.pallas import tpu as pltpu
from jax.sharding import PartitionSpec as P

MESH = pl.DeviceIdType.MESH
RING = 4
PLANE = RING * RING
ROWS = 48
NVIR = 4096
PIECE = RING * ROWS
HALF_PIECE = PIECE // 2
LEFT = 512
LEFT_CORE = LEFT // 2
RIGHT = 2048
COLS = RIGHT // 2
F32 = jnp.float32
BF16 = jnp.bfloat16


def device_of(y, x, z, c):
    return ((y % RING) * 8 + (x % RING) * 2 + (z % RING) // 2, (z % 2) * 2 + c)


def kernel(
    slabs, vir, occ, i_index, j_index, gamma,
    left_own, right_own, left, right_a, right_b, integrals, integrals_in, amplitude, vir_column,
    gamma_out, gamma_in,
    left_send, left_recv, spread_send, spread_recv, right_send, right_first, right_recv,
    core_send, core_recv, gamma_send, gamma_recv,
):
    aux, pan = lax.axis_index("aux"), lax.axis_index("pan")
    y, x = aux // 8, (aux // 2) % RING
    z, c = (aux % 2) * 2 + pan // 2, pan % 2
    rights = (right_a, right_b)

    def remote(src, dst, send, recv, to):
        copy = pltpu.make_async_remote_copy(
            src_ref=src, dst_ref=dst, send_sem=send, recv_sem=recv, device_id=to, device_id_type=MESH
        )
        copy.start()

    def wait(ref, sem):
        pltpu.make_async_copy(ref, ref, sem).wait()

    barrier = pltpu.get_barrier_semaphore()

    def greet(step, carry):
        pl.semaphore_signal(
            barrier, inc=1, device_id=device_of(y + step // 16, x + (step // 4) % 4, z + step % 4, c), device_id_type=MESH
        )
        return carry

    lax.fori_loop(1, 64, greet, 0)
    pl.semaphore_signal(barrier, inc=1, device_id=device_of(y, x, z, 1 - c), device_id_type=MESH)
    for slot in range(2):
        left_own[slot] = slabs[i_index[slot]]
        right_own[slot] = slabs[j_index[slot]]
    pl.semaphore_wait(barrier, 64)

    for dz in range(1, RING):
        to = (z + dz) % RING
        for half in range(2):
            remote(
                right_own.at[to // 2, :, pl.ds(pl.multiple_of((to % 2) * RIGHT + half * COLS, COLS), COLS)],
                rights[half].at[0, pl.ds(((-dz) % RING) * ROWS, ROWS)],
                right_send.at[half],
                right_first.at[half],
                device_of(y, x, z + dz, c),
            )
    for step in range(1, PLANE):
        spot = (step * 5) % PLANE
        dy, dx = spot // RING, spot % RING
        block = ((y + dy) % RING) * RING + (x + dx) % RING
        remote(
            left_own.at[block // 8, :, pl.ds(pl.multiple_of((block % 8) * LEFT, LEFT), LEFT)],
            left.at[((-dy) % RING) * RING + (-dx) % RING, pl.ds(0, ROWS)],
            left_send,
            left_recv,
            device_of(y + dy, x + dx, z, c),
        )
    own_block = y * RING + x
    left[0, 0:ROWS, :] = left_own[own_block // 8, :, pl.ds(pl.multiple_of((own_block % 8) * LEFT, LEFT), LEFT)]
    for half in range(2):
        rights[half][0, 0:ROWS, :] = right_own[
            z // 2, :, pl.ds(pl.multiple_of((z % 2) * RIGHT + half * COLS, COLS), COLS)
        ]

    def place(half, second, first):
        return second * RING + first if half == 0 else first * RING + second

    def toward(half, second, first):
        return device_of(y + second, x + first, z, c) if half == 0 else device_of(y + first, x + second, z, c)

    def send_first(half):
        for sign in (1, -1):
            spot = place(half, 0, (-sign) % RING)
            remote(
                rights[half].at[0], rights[half].at[spot], right_send.at[half], right_recv.at[half, spot, 0],
                toward(half, 0, sign),
            )

    def relay_first(half, sign):
        here, there = place(half, 0, (-sign) % RING), place(half, 0, 2)
        part = 0 if sign == 1 else 1
        rows = pl.ds(part * HALF_PIECE, HALF_PIECE)
        remote(
            rights[half].at[here, rows], rights[half].at[there, rows], right_send.at[half],
            right_recv.at[half, there, part], toward(half, 0, sign),
        )

    def send_second(half, first):
        here = place(half, 0, first)
        for sign in (1, -1):
            there = place(half, (-sign) % RING, first)
            remote(
                rights[half].at[here], rights[half].at[there], right_send.at[half], right_recv.at[half, there, 0],
                toward(half, sign, 0),
            )

    def relay_second(half, first, sign):
        here, there = place(half, (-sign) % RING, first), place(half, 2, first)
        part = 0 if sign == 1 else 1
        rows = pl.ds(part * HALF_PIECE, HALF_PIECE)
        remote(
            rights[half].at[here, rows], rights[half].at[there, rows], right_send.at[half],
            right_recv.at[half, there, part], toward(half, sign, 0),
        )

    def arrived(half, second, first):
        spot = place(half, second, first)
        if second == 2 or (second == 0 and first == 2):
            for part in range(2):
                wait(rights[half].at[spot, pl.ds(part * HALF_PIECE, HALF_PIECE)], right_recv.at[half, spot, part])
        else:
            wait(rights[half].at[spot], right_recv.at[half, spot, 0])

    ready = []

    def multiply(limit):
        for _ in range(min(limit, len(ready))):
            half, spot = ready.pop(0)

            def body(core, carry):
                columns = pl.ds(half * COLS, COLS)
                integrals[core, :, columns] += lax.dot_general(
                    left[spot, :, pl.ds(pl.multiple_of(core * LEFT_CORE, LEFT_CORE), LEFT_CORE)],
                    rights[half][spot],
                    (((0,), (0,)), ((), ())),
                    preferred_element_type=F32,
                )
                return carry

            lax.fori_loop(0, 2, body, 0)

    for half in range(2):
        wait(rights[half].at[0, pl.ds(ROWS, PIECE - ROWS)], right_first.at[half])
        send_first(half)
        send_second(half, 0)
        ready.append((half, 0))
    wait(left.at[pl.ds(0, PLANE - 1), pl.ds(0, ROWS)], left_recv)
    for dz in (2, 1, 3):
        remote(
            left.at[:, pl.ds(0, ROWS)], left.at[:, pl.ds(((-dz) % RING) * ROWS, ROWS)],
            spread_send, spread_recv.at[(-dz) % RING], device_of(y, x, z + dz, c),
        )
    integrals[...] = jnp.zeros_like(integrals)

    own_occ = occ[i_index[own_block // 8]] + occ[j_index[z // 2]]
    row_start = pl.multiple_of((own_block % 8) * LEFT + c * LEFT_CORE, LEFT_CORE)
    row = vir[:, pl.ds(row_start, LEFT_CORE)].astype(F32) - own_occ.astype(F32)
    vir_column[...] = jnp.transpose(jnp.broadcast_to(row, (128, LEFT_CORE)))

    for sign in (1, -1):
        for half in range(2):
            arrived(half, 0, (-sign) % RING)
            relay_first(half, sign)
            send_second(half, (-sign) % RING)
            ready.append((half, place(half, 0, (-sign) % RING)))
    for sign in (1, -1):
        for half in range(2):
            arrived(half, (-sign) % RING, 0)
            relay_second(half, 0, sign)
            ready.append((half, place(half, (-sign) % RING, 0)))
    for half in range(2):
        arrived(half, 0, 2)
        send_second(half, 2)
        ready.append((half, place(half, 0, 2)))
    for dz in range(1, RING):
        wait(left.at[:, pl.ds(dz * ROWS, ROWS)], spread_recv.at[dz])
    for first in (3, 1):
        for sign in (1, -1):
            for half in range(2):
                arrived(half, (-sign) % RING, first)
                relay_second(half, first, sign)
                ready.append((half, place(half, (-sign) % RING, first)))
                multiply(2)
    for half in range(2):
        arrived(half, 2, 0)
        ready.append((half, place(half, 2, 0)))
        multiply(2)
    for sign in (1, -1):
        for half in range(2):
            arrived(half, (-sign) % RING, 2)
            relay_second(half, 2, sign)
            ready.append((half, place(half, (-sign) % RING, 2)))
            multiply(2)
    for first in (3, 1):
        for half in range(2):
            arrived(half, 2, first)
            ready.append((half, place(half, 2, first)))
            multiply(2)
    multiply(len(ready))
    other = 1 - c
    for half in range(2):
        columns = pl.ds(half * COLS, COLS)
        arrived(half, 2, 2)
        ready.append((half, place(half, 2, 2)))
        multiply(1)
        remote(
            integrals.at[other, :, columns], integrals_in.at[:, columns], core_send.at[half], core_recv.at[half],
            device_of(y, x, z, other),
        )
    for half in range(2):
        columns = pl.ds(half * COLS, COLS)
        wait(integrals_in.at[:, columns], core_recv.at[half])

        def divide(tile, carry):
            start = pl.multiple_of(half * COLS + tile * 128, 128)
            tile_columns = pl.ds(start, 128)
            vir_row = vir[:, pl.ds(pl.multiple_of((z % 2) * RIGHT + start, 128), 128)].astype(F32)
            denominator = (vir_column[...] + vir_row) * (1.0 / 1024.0)
            total = integrals[c, :, tile_columns] + integrals_in[:, tile_columns]
            amplitude[c, :, tile_columns] = (total / denominator).astype(BF16)
            return carry

        lax.fori_loop(0, COLS // 128, divide, 0)
        remote(
            amplitude.at[c, :, columns], amplitude.at[c, :, columns], core_send.at[2 + half], core_recv.at[2 + half],
            device_of(y, x, z, other),
        )
    for half in range(2):
        wait(amplitude.at[other, :, pl.ds(half * COLS, COLS)], core_recv.at[2 + half])

    def back(step, carry):
        spot = ((step + 1) * 5) % PLANE
        dy, dx = spot // RING, spot % RING
        there = ((RING - dy) % RING) * RING + (RING - dx) % RING

        def body(core, inner):
            total = None
            for half in range(2):
                term = lax.dot_general(
                    rights[half][spot],
                    amplitude[core, :, half * COLS : (half + 1) * COLS],
                    (((1,), (1,)), ((), ())),
                    preferred_element_type=F32,
                )
                total = term if total is None else total + term
            gamma_out[spot, :, pl.ds(pl.multiple_of(core * LEFT_CORE, LEFT_CORE), LEFT_CORE)] = total.astype(BF16)
            return inner

        lax.fori_loop(0, 2, body, 0)
        for dz in (2, 1, 3):
            remote(
                gamma_out.at[spot, pl.ds(dz * ROWS, ROWS)],
                gamma_in.at[there, pl.ds(((-dz) % RING) * ROWS, ROWS)],
                gamma_send, gamma_recv.at[there], device_of(y + dy, x + dx, z + dz, c),
            )

        @pl.when(step < PLANE - 1)
        def _():
            remote(
                gamma_out.at[spot, pl.ds(0, ROWS)], gamma_in.at[there, pl.ds(0, ROWS)],
                gamma_send, gamma_recv.at[there], device_of(y + dy, x + dx, z, c),
            )

        return carry

    lax.fori_loop(0, PLANE, back, 0)
    gamma_in[0, 0:ROWS, :] = gamma_out[0, 0:ROWS, :]

    def add_up(spot):
        block = ((y + spot // RING) % RING) * RING + (x + spot % RING) % RING
        total = gamma_in[spot, 0:ROWS, :].astype(F32)
        for dz in range(1, RING):
            total = total + gamma_in[spot, dz * ROWS : (dz + 1) * ROWS, :].astype(F32)
        gamma[block // 8, :, pl.ds(pl.multiple_of((block % 8) * LEFT, LEFT), LEFT)] = total

    def finish(step, carry):
        sent = ((step + 1) * 5) % PLANE
        spot = ((RING - sent // RING) % RING) * RING + (RING - sent % RING) % RING
        wait(gamma_in.at[spot], gamma_recv.at[spot])
        add_up(spot)
        return carry

    lax.fori_loop(0, PLANE - 1, finish, 0)
    wait(gamma_in.at[0, pl.ds(ROWS, PIECE - ROWS)], gamma_recv.at[0])
    add_up(0)

    wait(left.at[pl.ds(0, PLANE - 1), pl.ds(0, ROWS)], left_send)
    wait(left.at[:, pl.ds(0, PIECE - ROWS)], spread_send)
    for half in range(2):
        wait(rights[half].at[0, pl.ds(0, PIECE - ROWS)], right_send.at[half])
        wait(rights[half].at[pl.ds(0, PLANE - 1)], right_send.at[half])
        columns = pl.ds(half * COLS, COLS)
        wait(integrals.at[other, :, columns], core_send.at[half])
        wait(amplitude.at[c, :, columns], core_send.at[2 + half])
    wait(gamma_out.at[pl.ds(0, PLANE - 1)], gamma_send)
    wait(gamma_out.at[0, pl.ds(0, PIECE - ROWS)], gamma_send)


def per_device(slabs, occ_energy, vir_energy, i_index, j_index):
    vmem = pl.BlockSpec(memory_space=pltpu.VMEM)
    smem = pl.BlockSpec(memory_space=pltpu.SMEM)
    dma = pltpu.SemaphoreType.DMA
    return pl.pallas_call(
        kernel,
        out_shape=jax.ShapeDtypeStruct((2, ROWS, NVIR), F32),
        in_specs=[vmem, vmem, smem, smem, smem],
        out_specs=vmem,
        scratch_shapes=[
            pltpu.VMEM((2, ROWS, NVIR), BF16),
            pltpu.VMEM((2, ROWS, NVIR), BF16),
            pltpu.VMEM((PLANE, PIECE, LEFT), BF16),
            pltpu.VMEM((PLANE, PIECE, COLS), BF16),
            pltpu.VMEM((PLANE, PIECE, COLS), BF16),
            pltpu.VMEM((2, LEFT_CORE, RIGHT), F32),
            pltpu.VMEM((LEFT_CORE, RIGHT), F32),
            pltpu.VMEM((2, LEFT_CORE, RIGHT), BF16),
            pltpu.VMEM((LEFT_CORE, 128), F32),
            pltpu.VMEM((PLANE, PIECE, LEFT), BF16),
            pltpu.VMEM((PLANE, PIECE, LEFT), BF16),
            dma, dma, dma, dma((RING,)), dma((2,)), dma((2,)), dma((2, PLANE, 2)),
            dma((4,)), dma((4,)), dma, dma((PLANE,)),
        ],
        compiler_params=pltpu.CompilerParams(
            collective_id=0, has_side_effects=True, vmem_limit_bytes=60 * 2**20
        ),
        name="back_transform",
    )(slabs, vir_energy.reshape(1, NVIR), occ_energy, i_index, j_index)


def solution(mesh):
    placed = (P(None, ("aux", "pan"), None), P(), P(), P(), P())
    return jax.shard_map(
        per_device,
        mesh=mesh,
        in_specs=placed,
        out_specs=P(None, ("aux", "pan"), None),
        check_vma=False,
    )
```

```python
import jax
import jax.numpy as jnp
from jax import lax
from jax.experimental import pallas as pl
from jax.experimental.pallas import tpu as pltpu
from jax.sharding import PartitionSpec as P

MESH = pl.DeviceIdType.MESH
RING = 4
PLANE = RING * RING
ROWS = 48
NVIR = 4096
PIECE = RING * ROWS
HALF_PIECE = PIECE // 2
LEFT = 512
LEFT_CORE = LEFT // 2
RIGHT = 2048
COLS = RIGHT // 2
F32 = jnp.float32
BF16 = jnp.bfloat16
LAG = 2


def device_of(y, x, z, c):
    return ((y % RING) * 8 + (x % RING) * 2 + (z % RING) // 2, (z % 2) * 2 + c)


def kernel(
    slabs, vir, occ, i_index, j_index, gamma,
    held, left_own, right_own, left, right_a, right_b, integrals, integrals_in, amplitude, vir_column,
    partial, opposite, relay, ring_out, ring_in, total_out,
    held_sem, left_send, left_recv, spread_send, spread_recv, right_send, right_first, right_recv,
    core_send, core_recv, opposite_send, relay_recv, ring_send, ring_recv, total_send, gamma_recv,
):
    aux, pan = lax.axis_index("aux"), lax.axis_index("pan")
    y, x = aux // 8, (aux // 2) % RING
    z, c = (aux % 2) * 2 + pan // 2, pan % 2
    rights = (right_a, right_b)

    def remote(src, dst, send, recv, to):
        copy = pltpu.make_async_remote_copy(
            src_ref=src, dst_ref=dst, send_sem=send, recv_sem=recv, device_id=to, device_id_type=MESH
        )
        copy.start()

    def wait(ref, sem):
        pltpu.make_async_copy(ref, ref, sem).wait()

    fetch = pltpu.make_async_copy(slabs, held, held_sem)
    fetch.start()
    barrier = pltpu.get_barrier_semaphore()

    def greet(*to):
        pl.semaphore_signal(barrier, inc=1, device_id=device_of(*to), device_id_type=MESH)

    for dz in range(1, RING):
        greet(y, x, z + dz, c)
    for spot in range(1, PLANE):
        greet(y + spot // RING, x + spot % RING, z, c)
    greet(y, x, z, 1 - c)
    fetch.wait()
    for slot in range(2):
        right_own[slot] = held[j_index[slot]]
    for slot in range(2):
        left_own[slot] = held[i_index[slot]]
    pl.semaphore_wait(barrier, RING - 1 + PLANE - 1 + 1)

    for dz in range(1, RING):
        to = (z + dz) % RING
        for half in range(2):
            remote(
                right_own.at[to // 2, :, pl.ds(pl.multiple_of((to % 2) * RIGHT + half * COLS, COLS), COLS)],
                rights[half].at[0, pl.ds(((-dz) % RING) * ROWS, ROWS)],
                right_send.at[half],
                right_first.at[half],
                device_of(y, x, z + dz, c),
            )
    for step in range(1, PLANE):
        spot = (step * 5) % PLANE
        dy, dx = spot // RING, spot % RING
        block = ((y + dy) % RING) * RING + (x + dx) % RING
        remote(
            left_own.at[block // 8, :, pl.ds(pl.multiple_of((block % 8) * LEFT, LEFT), LEFT)],
            left.at[((-dy) % RING) * RING + (-dx) % RING, pl.ds(0, ROWS)],
            left_send,
            left_recv,
            device_of(y + dy, x + dx, z, c),
        )
    own_block = y * RING + x
    left[0, 0:ROWS, :] = left_own[own_block // 8, :, pl.ds(pl.multiple_of((own_block % 8) * LEFT, LEFT), LEFT)]
    for half in range(2):
        rights[half][0, 0:ROWS, :] = right_own[
            z // 2, :, pl.ds(pl.multiple_of((z % 2) * RIGHT + half * COLS, COLS), COLS)
        ]

    def place(half, second, first):
        return second * RING + first if half == 0 else first * RING + second

    def toward(half, second, first):
        return device_of(y + second, x + first, z, c) if half == 0 else device_of(y + first, x + second, z, c)

    def send_first(half):
        for sign in (1, -1):
            spot = place(half, 0, (-sign) % RING)
            remote(
                rights[half].at[0], rights[half].at[spot], right_send.at[half], right_recv.at[half, spot, 0],
                toward(half, 0, sign),
            )

    def relay_first(half, sign):
        here, there = place(half, 0, (-sign) % RING), place(half, 0, 2)
        part = 0 if sign == 1 else 1
        rows = pl.ds(part * HALF_PIECE, HALF_PIECE)
        remote(
            rights[half].at[here, rows], rights[half].at[there, rows], right_send.at[half],
            right_recv.at[half, there, part], toward(half, 0, sign),
        )

    def send_second(half, first):
        here = place(half, 0, first)
        for sign in (1, -1):
            there = place(half, (-sign) % RING, first)
            remote(
                rights[half].at[here], rights[half].at[there], right_send.at[half], right_recv.at[half, there, 0],
                toward(half, sign, 0),
            )

    def relay_second(half, first, sign):
        here, there = place(half, (-sign) % RING, first), place(half, 2, first)
        part = 0 if sign == 1 else 1
        rows = pl.ds(part * HALF_PIECE, HALF_PIECE)
        remote(
            rights[half].at[here, rows], rights[half].at[there, rows], right_send.at[half],
            right_recv.at[half, there, part], toward(half, sign, 0),
        )

    def arrived(half, second, first):
        spot = place(half, second, first)
        if second == 2 or (second == 0 and first == 2):
            for part in range(2):
                wait(rights[half].at[spot, pl.ds(part * HALF_PIECE, HALF_PIECE)], right_recv.at[half, spot, part])
        else:
            wait(rights[half].at[spot], right_recv.at[half, spot, 0])

    ready = []

    def multiply(limit):
        for _ in range(min(limit, len(ready))):
            half, spot = ready.pop(0)

            def body(core, carry):
                columns = pl.ds(half * COLS, COLS)
                integrals[core, :, columns] += lax.dot_general(
                    left[spot, :, pl.ds(pl.multiple_of(core * LEFT_CORE, LEFT_CORE), LEFT_CORE)],
                    rights[half][spot],
                    (((0,), (0,)), ((), ())),
                    preferred_element_type=F32,
                )
                return carry

            lax.fori_loop(0, 2, body, 0)

    for half in range(2):
        wait(rights[half].at[0, pl.ds(ROWS, PIECE - ROWS)], right_first.at[half])
        send_first(half)
        send_second(half, 0)
        ready.append((half, 0))
    wait(left.at[pl.ds(0, PLANE - 1), pl.ds(0, ROWS)], left_recv)
    for dz in (2, 1, 3):
        remote(
            left.at[:, pl.ds(0, ROWS)], left.at[:, pl.ds(((-dz) % RING) * ROWS, ROWS)],
            spread_send, spread_recv.at[(-dz) % RING], device_of(y, x, z + dz, c),
        )
    integrals[...] = jnp.zeros_like(integrals)

    own_occ = occ[i_index[own_block // 8]] + occ[j_index[z // 2]]
    row_start = pl.multiple_of((own_block % 8) * LEFT + c * LEFT_CORE, LEFT_CORE)
    row = vir[:, pl.ds(row_start, LEFT_CORE)].astype(F32) - own_occ.astype(F32)
    vir_column[...] = jnp.transpose(jnp.broadcast_to(row, (128, LEFT_CORE)))

    for sign in (1, -1):
        for half in range(2):
            arrived(half, 0, (-sign) % RING)
            relay_first(half, sign)
            send_second(half, (-sign) % RING)
            ready.append((half, place(half, 0, (-sign) % RING)))
    for sign in (1, -1):
        for half in range(2):
            arrived(half, (-sign) % RING, 0)
            relay_second(half, 0, sign)
            ready.append((half, place(half, (-sign) % RING, 0)))
    for half in range(2):
        arrived(half, 0, 2)
        send_second(half, 2)
        ready.append((half, place(half, 0, 2)))
    for dz in range(1, RING):
        wait(left.at[:, pl.ds(dz * ROWS, ROWS)], spread_recv.at[dz])
    for first in (3, 1):
        for sign in (1, -1):
            for half in range(2):
                arrived(half, (-sign) % RING, first)
                relay_second(half, first, sign)
                ready.append((half, place(half, (-sign) % RING, first)))
                multiply(2)
    for half in range(2):
        arrived(half, 2, 0)
        ready.append((half, place(half, 2, 0)))
        multiply(2)
    for sign in (1, -1):
        for half in range(2):
            arrived(half, (-sign) % RING, 2)
            relay_second(half, 2, sign)
            ready.append((half, place(half, (-sign) % RING, 2)))
            multiply(2)
    for first in (3, 1):
        for half in range(2):
            arrived(half, 2, first)
            ready.append((half, place(half, 2, first)))
            multiply(2)
    multiply(len(ready))
    other = 1 - c
    for half in range(2):
        columns = pl.ds(half * COLS, COLS)
        arrived(half, 2, 2)
        ready.append((half, place(half, 2, 2)))
        multiply(1)
        remote(
            integrals.at[other, :, columns], integrals_in.at[:, columns], core_send.at[half], core_recv.at[half],
            device_of(y, x, z, other),
        )
    for half in range(2):
        columns = pl.ds(half * COLS, COLS)
        wait(integrals_in.at[:, columns], core_recv.at[half])

        def divide(tile, carry):
            start = pl.multiple_of(half * COLS + tile * 128, 128)
            tile_columns = pl.ds(start, 128)
            vir_row = vir[:, pl.ds(pl.multiple_of((z % 2) * RIGHT + start, 128), 128)].astype(F32)
            denominator = (vir_column[...] + vir_row) * (1.0 / 1024.0)
            total = integrals[c, :, tile_columns] + integrals_in[:, tile_columns]
            amplitude[c, :, tile_columns] = (total / denominator).astype(BF16)
            return carry

        lax.fori_loop(0, COLS // 128, divide, 0)
        remote(
            amplitude.at[c, :, columns], amplitude.at[c, :, columns], core_send.at[2 + half], core_recv.at[2 + half],
            device_of(y, x, z, other),
        )
    for half in range(2):
        wait(amplitude.at[other, :, pl.ds(half * COLS, COLS)], core_recv.at[2 + half])

    near, far = pl.ds(0, LEFT_CORE), pl.ds(LEFT_CORE, LEFT_CORE)

    def order(step):
        return ((step + 1) * 5) % PLANE

    def multiply_back(spot):
        def body(core, carry):
            columns = pl.ds(pl.multiple_of(core * LEFT_CORE, LEFT_CORE), LEFT_CORE)
            total = None
            for half in range(2):
                term = lax.dot_general(
                    rights[half][spot],
                    amplitude[core, :, half * COLS : (half + 1) * COLS],
                    (((1,), (1,)), ((), ())),
                    preferred_element_type=F32,
                )
                total = term if total is None else total + term
            partial[spot, :, columns] = total
            opposite[spot, :, columns] = total[2 * ROWS : 3 * ROWS].astype(BF16)
            return carry

        lax.fori_loop(0, 2, body, 0)
        for columns, dz in ((near, 1), (far, -1)):
            remote(
                opposite.at[spot, :, columns], relay.at[spot, :, columns], opposite_send, relay_recv.at[spot],
                device_of(y, x, z + dz, c),
            )

    def pass_on(spot):
        wait(relay.at[spot], relay_recv.at[spot])
        ring_out[spot, 0, :, near] = (partial[spot, ROWS : 2 * ROWS, near] + relay[spot, :, near].astype(F32)).astype(BF16)
        ring_out[spot, 0, :, far] = partial[spot, ROWS : 2 * ROWS, far].astype(BF16)
        ring_out[spot, 1, :, near] = partial[spot, 3 * ROWS :, near].astype(BF16)
        ring_out[spot, 1, :, far] = (partial[spot, 3 * ROWS :, far] + relay[spot, :, far].astype(F32)).astype(BF16)
        for way, dz in ((0, 1), (1, -1)):
            remote(
                ring_out.at[spot, way], ring_in.at[spot, way], ring_send, ring_recv.at[spot], device_of(y, x, z + dz, c)
            )

    own_columns = pl.ds(pl.multiple_of((own_block % 8) * LEFT, LEFT), LEFT)

    def hand_over(spot):
        wait(ring_in.at[spot], ring_recv.at[spot])
        total_out[spot] = partial[spot, 0:ROWS] + ring_in[spot, 0].astype(F32) + ring_in[spot, 1].astype(F32)

    def back(step, carry):
        @pl.when(step < PLANE)
        def _():
            multiply_back(order(step))

        @pl.when((step >= LAG) & (step < PLANE + LAG))
        def _():
            pass_on(order(step - LAG))

        @pl.when(step >= 2 * LAG)
        def _():
            spot = order(step - 2 * LAG)
            hand_over(spot)

            @pl.when(step < PLANE + 2 * LAG - 1)
            def _():
                remote(
                    total_out.at[spot], gamma.at[own_block // 8, :, own_columns], total_send, gamma_recv,
                    device_of(y + spot // RING, x + spot % RING, z, c),
                )

        return carry

    lax.fori_loop(0, PLANE + 2 * LAG, back, 0)
    keep = pltpu.make_async_copy(total_out.at[0], gamma.at[own_block // 8, :, own_columns], held_sem)
    keep.start()
    keep.wait()
    wait(total_out.at[pl.ds(0, PLANE - 1)], gamma_recv)

    wait(left.at[pl.ds(0, PLANE - 1), pl.ds(0, ROWS)], left_send)
    wait(left.at[:, pl.ds(0, PIECE - ROWS)], spread_send)
    for half in range(2):
        wait(rights[half].at[0, pl.ds(0, PIECE - ROWS)], right_send.at[half])
        wait(rights[half].at[pl.ds(0, PLANE - 1)], right_send.at[half])
        columns = pl.ds(half * COLS, COLS)
        wait(integrals.at[other, :, columns], core_send.at[half])
        wait(amplitude.at[c, :, columns], core_send.at[2 + half])
    wait(opposite, opposite_send)
    wait(ring_out, ring_send)
    wait(total_out.at[pl.ds(0, PLANE - 1)], total_send)


def per_device(slabs, occ_energy, vir_energy, i_index, j_index):
    vmem = pl.BlockSpec(memory_space=pltpu.VMEM)
    anywhere = pl.BlockSpec(memory_space=pl.ANY)
    smem = pl.BlockSpec(memory_space=pltpu.SMEM)
    dma = pltpu.SemaphoreType.DMA
    return pl.pallas_call(
        kernel,
        out_shape=jax.ShapeDtypeStruct((2, ROWS, NVIR), F32),
        in_specs=[anywhere, vmem, smem, smem, smem],
        out_specs=anywhere,
        scratch_shapes=[
            pltpu.VMEM((8, ROWS, NVIR), BF16),
            pltpu.VMEM((2, ROWS, NVIR), BF16),
            pltpu.VMEM((2, ROWS, NVIR), BF16),
            pltpu.VMEM((PLANE, PIECE, LEFT), BF16),
            pltpu.VMEM((PLANE, PIECE, COLS), BF16),
            pltpu.VMEM((PLANE, PIECE, COLS), BF16),
            pltpu.VMEM((2, LEFT_CORE, RIGHT), F32),
            pltpu.VMEM((LEFT_CORE, RIGHT), F32),
            pltpu.VMEM((2, LEFT_CORE, RIGHT), BF16),
            pltpu.VMEM((LEFT_CORE, 128), F32),
            pltpu.VMEM((PLANE, PIECE, LEFT), F32),
            pltpu.VMEM((PLANE, ROWS, LEFT), BF16),
            pltpu.VMEM((PLANE, ROWS, LEFT), BF16),
            pltpu.VMEM((PLANE, 2, ROWS, LEFT), BF16),
            pltpu.VMEM((PLANE, 2, ROWS, LEFT), BF16),
            pltpu.VMEM((PLANE, ROWS, LEFT), F32),
            dma, dma, dma, dma, dma((RING,)), dma((2,)), dma((2,)), dma((2, PLANE, 2)),
            dma((4,)), dma((4,)), dma, dma((PLANE,)), dma, dma((PLANE,)), dma, dma,
        ],
        compiler_params=pltpu.CompilerParams(
            collective_id=0, has_side_effects=True, vmem_limit_bytes=60 * 2**20
        ),
        name="back_transform",
    )(slabs, vir_energy.reshape(1, NVIR), occ_energy, i_index, j_index)


def solution(mesh):
    placed = (P(None, ("aux", "pan"), None), P(), P(), P(), P())
    return jax.shard_map(
        per_device,
        mesh=mesh,
        in_specs=placed,
        out_specs=P(None, ("aux", "pan"), None),
        check_vma=False,
    )
```

```python
import jax
import jax.numpy as jnp
from jax import lax
from jax.experimental import pallas as pl
from jax.experimental.pallas import tpu as pltpu
from jax.sharding import PartitionSpec as P

MESH = pl.DeviceIdType.MESH
RING = 4
PLANE = RING * RING
ROWS = 48
NVIR = 4096
PIECE = RING * ROWS
HALF_PIECE = PIECE // 2
LEFT = 512
LEFT_CORE = LEFT // 2
RIGHT = 2048
COLS = RIGHT // 2
F32 = jnp.float32
BF16 = jnp.bfloat16
LAG = 4
ORDER = (10, 9, 11, 6, 14, 5, 15, 7, 13, 2, 8, 1, 3, 4, 12, 0)


def device_of(y, x, z, c):
    return ((y % RING) * 8 + (x % RING) * 2 + (z % RING) // 2, (z % 2) * 2 + c)


def kernel(
    slabs, vir, occ, i_index, j_index, gamma,
    held, left_own, right_own, left, right_a, right_b, integrals, integrals_in, amplitude, vir_column,
    partial, opposite, relay, ring_out, ring_in, total_out,
    held_sem, left_send, left_recv, spread_send, spread_recv, right_send, right_first, right_recv,
    core_send, core_recv, opposite_send, relay_recv, ring_send, ring_recv, total_send, gamma_recv,
):
    aux, pan = lax.axis_index("aux"), lax.axis_index("pan")
    y, x = aux // 8, (aux // 2) % RING
    z, c = (aux % 2) * 2 + pan // 2, pan % 2
    rights = (right_a, right_b)

    def remote(src, dst, send, recv, to):
        copy = pltpu.make_async_remote_copy(
            src_ref=src, dst_ref=dst, send_sem=send, recv_sem=recv, device_id=to, device_id_type=MESH
        )
        copy.start()

    def wait(ref, sem):
        pltpu.make_async_copy(ref, ref, sem).wait()

    fetch = pltpu.make_async_copy(slabs, held, held_sem)
    fetch.start()
    barrier = pltpu.get_barrier_semaphore()

    def greet(*to):
        pl.semaphore_signal(barrier, inc=1, device_id=device_of(*to), device_id_type=MESH)

    for dz in range(1, RING):
        greet(y, x, z + dz, c)
    for spot in range(1, PLANE):
        greet(y + spot // RING, x + spot % RING, z, c)
    greet(y, x, z, 1 - c)
    fetch.wait()
    for slot in range(2):
        right_own[slot] = held[j_index[slot]]
    for slot in range(2):
        left_own[slot] = held[i_index[slot]]
    pl.semaphore_wait(barrier, RING - 1 + PLANE - 1 + 1)

    for dz in range(1, RING):
        to = (z + dz) % RING
        for half in range(2):
            remote(
                right_own.at[to // 2, :, pl.ds(pl.multiple_of((to % 2) * RIGHT + half * COLS, COLS), COLS)],
                rights[half].at[0, pl.ds(((-dz) % RING) * ROWS, ROWS)],
                right_send.at[half],
                right_first.at[half],
                device_of(y, x, z + dz, c),
            )
    def place(half, second, first):
        return second * RING + first if half == 0 else first * RING + second

    def toward(half, second, first):
        return device_of(y + second, x + first, z, c) if half == 0 else device_of(y + first, x + second, z, c)

    def send_first(half, rows):
        for sign in (1, -1):
            spot = place(half, 0, (-sign) % RING)
            remote(
                rights[half].at[0, rows], rights[half].at[spot, rows], right_send.at[half],
                right_recv.at[half, spot, 0], toward(half, 0, sign),
            )

    def relay_first(half, sign):
        here, there = place(half, 0, (-sign) % RING), place(half, 0, 2)
        part = 0 if sign == 1 else 1
        rows = pl.ds(part * HALF_PIECE, HALF_PIECE)
        remote(
            rights[half].at[here, rows], rights[half].at[there, rows], right_send.at[half],
            right_recv.at[half, there, part], toward(half, 0, sign),
        )

    def send_second(half, first, rows=pl.ds(0, PIECE)):
        here = place(half, 0, first)
        for sign in (1, -1):
            there = place(half, (-sign) % RING, first)
            remote(
                rights[half].at[here, rows], rights[half].at[there, rows], right_send.at[half],
                right_recv.at[half, there, 0], toward(half, sign, 0),
            )

    def relay_second(half, first, sign):
        here, there = place(half, (-sign) % RING, first), place(half, 2, first)
        part = 0 if sign == 1 else 1
        rows = pl.ds(part * HALF_PIECE, HALF_PIECE)
        remote(
            rights[half].at[here, rows], rights[half].at[there, rows], right_send.at[half],
            right_recv.at[half, there, part], toward(half, sign, 0),
        )

    def arrived(half, second, first):
        spot = place(half, second, first)
        if second == 2 or (second == 0 and first == 2):
            for part in range(2):
                wait(rights[half].at[spot, pl.ds(part * HALF_PIECE, HALF_PIECE)], right_recv.at[half, spot, part])
        else:
            wait(rights[half].at[spot], right_recv.at[half, spot, 0])

    ready = []

    def multiply(limit):
        for _ in range(min(limit, len(ready))):
            half, spot = ready.pop(0)

            def body(core, carry):
                columns = pl.ds(half * COLS, COLS)
                integrals[core, :, columns] += lax.dot_general(
                    left[spot, :, pl.ds(pl.multiple_of(core * LEFT_CORE, LEFT_CORE), LEFT_CORE)],
                    rights[half][spot],
                    (((0,), (0,)), ((), ())),
                    preferred_element_type=F32,
                )
                return carry

            lax.fori_loop(0, 2, body, 0)

    for half in range(2):
        rights[half][0, 0:ROWS, :] = right_own[
            z // 2, :, pl.ds(pl.multiple_of((z % 2) * RIGHT + half * COLS, COLS), COLS)
        ]
        send_first(half, pl.ds(0, ROWS))
        send_second(half, 0, pl.ds(0, ROWS))

    for step in range(1, PLANE):
        spot = (step * 5) % PLANE
        dy, dx = spot // RING, spot % RING
        block = ((y + dy) % RING) * RING + (x + dx) % RING
        remote(
            left_own.at[block // 8, :, pl.ds(pl.multiple_of((block % 8) * LEFT, LEFT), LEFT)],
            left.at[((-dy) % RING) * RING + (-dx) % RING, pl.ds(0, ROWS)],
            left_send,
            left_recv,
            device_of(y + dy, x + dx, z, c),
        )
    own_block = y * RING + x
    left[0, 0:ROWS, :] = left_own[own_block // 8, :, pl.ds(pl.multiple_of((own_block % 8) * LEFT, LEFT), LEFT)]

    rest = pl.ds(ROWS, PIECE - ROWS)
    for half in range(2):
        wait(rights[half].at[0, rest], right_first.at[half])
        send_first(half, rest)
        send_second(half, 0, rest)
        ready.append((half, 0))
    wait(left.at[pl.ds(0, PLANE - 1), pl.ds(0, ROWS)], left_recv)
    for dz in (2, 1, 3):
        remote(
            left.at[:, pl.ds(0, ROWS)], left.at[:, pl.ds(((-dz) % RING) * ROWS, ROWS)],
            spread_send, spread_recv.at[(-dz) % RING], device_of(y, x, z + dz, c),
        )
    integrals[...] = jnp.zeros_like(integrals)

    own_occ = occ[i_index[own_block // 8]] + occ[j_index[z // 2]]
    row_start = pl.multiple_of((own_block % 8) * LEFT + c * LEFT_CORE, LEFT_CORE)
    row = vir[:, pl.ds(row_start, LEFT_CORE)].astype(F32) - own_occ.astype(F32)
    vir_column[...] = jnp.transpose(jnp.broadcast_to(row, (128, LEFT_CORE)))

    for sign in (1, -1):
        for half in range(2):
            arrived(half, 0, (-sign) % RING)
            relay_first(half, sign)
            send_second(half, (-sign) % RING)
            ready.append((half, place(half, 0, (-sign) % RING)))
    for sign in (1, -1):
        for half in range(2):
            arrived(half, (-sign) % RING, 0)
            relay_second(half, 0, sign)
            ready.append((half, place(half, (-sign) % RING, 0)))
    for half in range(2):
        arrived(half, 0, 2)
        send_second(half, 2)
        ready.append((half, place(half, 0, 2)))
    for dz in range(1, RING):
        wait(left.at[:, pl.ds(dz * ROWS, ROWS)], spread_recv.at[dz])
    for first in (3, 1):
        for sign in (1, -1):
            for half in range(2):
                arrived(half, (-sign) % RING, first)
                relay_second(half, first, sign)
                ready.append((half, place(half, (-sign) % RING, first)))
                multiply(2)
    for half in range(2):
        arrived(half, 2, 0)
        ready.append((half, place(half, 2, 0)))
        multiply(2)
    for sign in (1, -1):
        for half in range(2):
            arrived(half, (-sign) % RING, 2)
            relay_second(half, 2, sign)
            ready.append((half, place(half, (-sign) % RING, 2)))
            multiply(2)
    for first in (3, 1):
        for half in range(2):
            arrived(half, 2, first)
            ready.append((half, place(half, 2, first)))
            multiply(2)
    multiply(len(ready))
    other = 1 - c
    for half in range(2):
        columns = pl.ds(half * COLS, COLS)
        arrived(half, 2, 2)
        ready.append((half, place(half, 2, 2)))
        multiply(1)
        remote(
            integrals.at[other, :, columns], integrals_in.at[:, columns], core_send.at[half], core_recv.at[half],
            device_of(y, x, z, other),
        )
    for half in range(2):
        columns = pl.ds(half * COLS, COLS)
        wait(integrals_in.at[:, columns], core_recv.at[half])

        def divide(tile, carry):
            start = pl.multiple_of(half * COLS + tile * 128, 128)
            tile_columns = pl.ds(start, 128)
            vir_row = vir[:, pl.ds(pl.multiple_of((z % 2) * RIGHT + start, 128), 128)].astype(F32)
            denominator = (vir_column[...] + vir_row) * (1.0 / 1024.0)
            total = integrals[c, :, tile_columns] + integrals_in[:, tile_columns]
            amplitude[c, :, tile_columns] = (total / denominator).astype(BF16)
            return carry

        lax.fori_loop(0, COLS // 128, divide, 0)
        remote(
            amplitude.at[c, :, columns], amplitude.at[c, :, columns], core_send.at[2 + half], core_recv.at[2 + half],
            device_of(y, x, z, other),
        )
    near, far = pl.ds(0, LEFT_CORE), pl.ds(LEFT_CORE, LEFT_CORE)

    def order(step):
        spot = step * 0
        for index, entry in enumerate(ORDER):
            spot = jnp.where(step == index, entry, spot)
        return spot

    def multiply_back(step, spot):
        def body(turn, carry):
            core = (c + turn) % 2

            @pl.when((step == 0) & (turn == 1))
            def _():
                for half in range(2):
                    wait(amplitude.at[other, :, pl.ds(half * COLS, COLS)], core_recv.at[2 + half])

            columns = pl.ds(pl.multiple_of(core * LEFT_CORE, LEFT_CORE), LEFT_CORE)
            total = None
            for half in range(2):
                term = lax.dot_general(
                    rights[half][spot],
                    amplitude[core, :, half * COLS : (half + 1) * COLS],
                    (((1,), (1,)), ((), ())),
                    preferred_element_type=F32,
                )
                total = term if total is None else total + term
            partial[spot, :, columns] = total
            opposite[spot, core] = total[2 * ROWS : 3 * ROWS].astype(BF16)
            return carry

        lax.fori_loop(0, 2, body, 0)
        for way, dz in ((0, 1), (1, -1)):
            remote(
                opposite.at[spot, way], relay.at[spot, way], opposite_send, relay_recv.at[spot],
                device_of(y, x, z + dz, c),
            )

    def pass_on(spot):
        wait(relay.at[spot], relay_recv.at[spot])
        ring_out[spot, 0, :, near] = (partial[spot, ROWS : 2 * ROWS, near] + relay[spot, 0].astype(F32)).astype(BF16)
        ring_out[spot, 0, :, far] = partial[spot, ROWS : 2 * ROWS, far].astype(BF16)
        ring_out[spot, 1, :, near] = partial[spot, 3 * ROWS :, near].astype(BF16)
        ring_out[spot, 1, :, far] = (partial[spot, 3 * ROWS :, far] + relay[spot, 1].astype(F32)).astype(BF16)
        for way, dz in ((0, 1), (1, -1)):
            remote(
                ring_out.at[spot, way], ring_in.at[spot, way], ring_send, ring_recv.at[spot], device_of(y, x, z + dz, c)
            )

    own_columns = pl.ds(pl.multiple_of((own_block % 8) * LEFT, LEFT), LEFT)

    def hand_over(spot):
        wait(ring_in.at[spot], ring_recv.at[spot])
        total_out[spot] = partial[spot, 0:ROWS] + ring_in[spot, 0].astype(F32) + ring_in[spot, 1].astype(F32)

    def back(step, carry):
        @pl.when(step < PLANE)
        def _():
            multiply_back(step, order(step))

        @pl.when((step >= LAG) & (step < PLANE + LAG))
        def _():
            pass_on(order(step - LAG))

        @pl.when(step >= 2 * LAG)
        def _():
            spot = order(step - 2 * LAG)
            hand_over(spot)

            @pl.when(step < PLANE + 2 * LAG - 1)
            def _():
                remote(
                    total_out.at[spot], gamma.at[own_block // 8, :, own_columns], total_send, gamma_recv,
                    device_of(y + spot // RING, x + spot % RING, z, c),
                )

        return carry

    lax.fori_loop(0, PLANE + 2 * LAG, back, 0)
    keep = pltpu.make_async_copy(total_out.at[0], gamma.at[own_block // 8, :, own_columns], held_sem)
    keep.start()
    keep.wait()
    wait(total_out.at[pl.ds(0, PLANE - 1)], gamma_recv)

    wait(left.at[pl.ds(0, PLANE - 1), pl.ds(0, ROWS)], left_send)
    wait(left.at[:, pl.ds(0, PIECE - ROWS)], spread_send)
    for half in range(2):
        wait(rights[half].at[0, pl.ds(0, PIECE - ROWS)], right_send.at[half])
        wait(rights[half].at[pl.ds(0, PLANE - 1)], right_send.at[half])
        columns = pl.ds(half * COLS, COLS)
        wait(integrals.at[other, :, columns], core_send.at[half])
        wait(amplitude.at[c, :, columns], core_send.at[2 + half])
    wait(opposite, opposite_send)
    wait(ring_out, ring_send)
    wait(total_out.at[pl.ds(0, PLANE - 1)], total_send)


def copy_kernel(source, target, held, sem):
    parts = [(n, pl.ds(row, 8), row // 8) for n in range(2) for row in range(0, ROWS, 8)]
    reads = [pltpu.make_async_copy(source.at[n, rows], held.at[n, rows], sem.at[0, n, k]) for n, rows, k in parts]
    writes = [pltpu.make_async_copy(held.at[n, rows], target.at[n, rows], sem.at[1, n, k]) for n, rows, k in parts]
    for read in reads:
        read.start()
    for read, write in zip(reads, writes):
        read.wait()
        write.start()
    for write in writes:
        write.wait()


def per_device(slabs, occ_energy, vir_energy, i_index, j_index):
    vmem = pl.BlockSpec(memory_space=pltpu.VMEM)
    anywhere = pl.BlockSpec(memory_space=pl.ANY)
    smem = pl.BlockSpec(memory_space=pltpu.SMEM)
    dma = pltpu.SemaphoreType.DMA
    gamma = pl.pallas_call(
        kernel,
        out_shape=jax.ShapeDtypeStruct((2, ROWS, NVIR), F32),
        in_specs=[anywhere, vmem, smem, smem, smem],
        out_specs=anywhere,
        scratch_shapes=[
            pltpu.VMEM((8, ROWS, NVIR), BF16),
            pltpu.VMEM((2, ROWS, NVIR), BF16),
            pltpu.VMEM((2, ROWS, NVIR), BF16),
            pltpu.VMEM((PLANE, PIECE, LEFT), BF16),
            pltpu.VMEM((PLANE, PIECE, COLS), BF16),
            pltpu.VMEM((PLANE, PIECE, COLS), BF16),
            pltpu.VMEM((2, LEFT_CORE, RIGHT), F32),
            pltpu.VMEM((LEFT_CORE, RIGHT), F32),
            pltpu.VMEM((2, LEFT_CORE, RIGHT), BF16),
            pltpu.VMEM((LEFT_CORE, 128), F32),
            pltpu.VMEM((PLANE, PIECE, LEFT), F32),
            pltpu.VMEM((PLANE, 2, ROWS, LEFT_CORE), BF16),
            pltpu.VMEM((PLANE, 2, ROWS, LEFT_CORE), BF16),
            pltpu.VMEM((PLANE, 2, ROWS, LEFT), BF16),
            pltpu.VMEM((PLANE, 2, ROWS, LEFT), BF16),
            pltpu.VMEM((PLANE, ROWS, LEFT), F32),
            dma, dma, dma, dma, dma((RING,)), dma((2,)), dma((2,)), dma((2, PLANE, 2)),
            dma((4,)), dma((4,)), dma, dma((PLANE,)), dma, dma((PLANE,)), dma, dma,
        ],
        compiler_params=pltpu.CompilerParams(
            collective_id=0, has_side_effects=True, vmem_limit_bytes=60 * 2**20
        ),
        name="back_transform",
    )(slabs, vir_energy.reshape(1, NVIR), occ_energy, i_index, j_index)
    return pl.pallas_call(
        copy_kernel,
        out_shape=jax.ShapeDtypeStruct((2, ROWS, NVIR), F32),
        in_specs=[anywhere],
        out_specs=anywhere,
        scratch_shapes=[pltpu.VMEM((2, ROWS, NVIR), F32), dma((2, 2, ROWS // 8))],
        name="result",
    )(gamma)


def solution(mesh):
    placed = (P(None, ("aux", "pan"), None), P(), P(), P(), P())
    return jax.shard_map(
        per_device,
        mesh=mesh,
        in_specs=placed,
        out_specs=P(None, ("aux", "pan"), None),
        check_vma=False,
    )
```

```python
import jax
import jax.numpy as jnp
from jax import lax
from jax.experimental import pallas as pl
from jax.experimental.pallas import tpu as pltpu
from jax.sharding import PartitionSpec as P

MESH = pl.DeviceIdType.MESH
RING = 4
PLANE = RING * RING
ROWS = 48
NVIR = 4096
PIECE = RING * ROWS
HALF_PIECE = PIECE // 2
LEFT = 512
LEFT_CORE = LEFT // 2
RIGHT = 2048
COLS = RIGHT // 2
F32 = jnp.float32
BF16 = jnp.bfloat16
LAG = 4
RANK = (0, 1, 3, 2)
ORDER = (10, 9, 11, 6, 14, 5, 15, 7, 13, 2, 8, 1, 3, 4, 12, 0)


def device_of(y, x, z, c):
    return ((y % RING) * 8 + (x % RING) * 2 + (z % RING) // 2, (z % 2) * 2 + c)


def rows_of(dz):
    return pl.ds(RANK[dz % RING] * ROWS, ROWS)


def kernel(
    slabs, vir, occ, i_index, j_index, gamma,
    held, left_own, right_own, left, left_all, right_a, right_b, integrals, amplitude, vir_column,
    partial, opposite, relay, ring_out, ring_in, total_out,
    held_sem, left_send, left_recv, spread_send, spread_recv, core_left, right_send, right_first, right_recv,
    core_send, core_recv, opposite_send, relay_recv, ring_send, ring_recv, total_send, gamma_recv,
):
    aux, pan = lax.axis_index("aux"), lax.axis_index("pan")
    y, x = aux // 8, (aux // 2) % RING
    z, c = (aux % 2) * 2 + pan // 2, pan % 2
    other = 1 - c
    sibling = device_of(y, x, z, other)
    rights = (right_a, right_b)
    own_block = y * RING + x

    def remote(src, dst, send, recv, to):
        copy = pltpu.make_async_remote_copy(
            src_ref=src, dst_ref=dst, send_sem=send, recv_sem=recv, device_id=to, device_id_type=MESH
        )
        copy.start()

    def wait(ref, sem):
        pltpu.make_async_copy(ref, ref, sem).wait()

    fetch = pltpu.make_async_copy(slabs, held, held_sem)
    fetch.start()
    barrier = pltpu.get_barrier_semaphore()

    def greet(to):
        pl.semaphore_signal(barrier, inc=1, device_id=to, device_id_type=MESH)

    for dz in range(1, RING):
        greet(device_of(y, x, z + dz, c))
    greet(sibling)
    for spot in range(1, PLANE):
        for core in range(2):
            greet(device_of(y + spot // RING, x + spot % RING, z, core))
    fetch.wait()
    for slot in range(2):
        right_own[slot] = held[j_index[slot]]
    for slot in range(2):
        left_own[slot] = held[i_index[slot]]
    pl.semaphore_wait(barrier, RING - 1 + 1 + 2 * (PLANE - 1))

    def right_columns(to, half):
        return right_own.at[to // 2, :, pl.ds(pl.multiple_of((to % 2) * RIGHT + half * COLS, COLS), COLS)]

    def exchange(dz, half):
        remote(
            right_columns((z + dz) % RING, half), rights[half].at[c, 0, rows_of(-dz)], right_send.at[half],
            right_first.at[half, 1 if dz == 2 else 0], device_of(y, x, z + dz, c),
        )

    def place(half, second, first):
        return second * RING + first if half == 0 else first * RING + second

    def toward(half, second, first):
        return device_of(y + second, x + first, z, c) if half == 0 else device_of(y + first, x + second, z, c)

    def send_first(half, rows, part):
        for sign in (1, -1):
            spot = place(half, 0, (-sign) % RING)
            remote(
                rights[half].at[c, 0, rows], rights[half].at[c, spot, rows], right_send.at[half],
                right_recv.at[half, spot, part], toward(half, 0, sign),
            )

    def relay_first(half, sign):
        here, there = place(half, 0, (-sign) % RING), place(half, 0, 2)
        part = 0 if sign == 1 else 1
        rows = pl.ds(part * HALF_PIECE, HALF_PIECE)
        remote(
            rights[half].at[c, here, rows], rights[half].at[c, there, rows], right_send.at[half],
            right_recv.at[half, there, part], toward(half, 0, sign),
        )

    def send_second(half, first, rows=pl.ds(0, PIECE)):
        here = place(half, 0, first)
        for sign in (1, -1):
            there = place(half, (-sign) % RING, first)
            remote(
                rights[half].at[c, here, rows], rights[half].at[c, there, rows], right_send.at[half],
                right_recv.at[half, there, 0], toward(half, sign, 0),
            )

    def relay_second(half, first, sign):
        here, there = place(half, (-sign) % RING, first), place(half, 2, first)
        part = 0 if sign == 1 else 1
        rows = pl.ds(part * HALF_PIECE, HALF_PIECE)
        remote(
            rights[half].at[c, here, rows], rights[half].at[c, there, rows], right_send.at[half],
            right_recv.at[half, there, part], toward(half, sign, 0),
        )

    def arrived(half, second, first):
        spot = place(half, second, first)
        if second == 2 or (second == 0 and first == 2):
            for part in range(2):
                wait(rights[half].at[c, spot, pl.ds(part * HALF_PIECE, HALF_PIECE)], right_recv.at[half, spot, part])
        else:
            wait(rights[half].at[c, spot], right_recv.at[half, spot, 0])

    ready = []

    def share(half, spot):
        block = rights[half].at[c, spot]
        remote(block, block, core_send.at[half], core_recv.at[half, spot], sibling)
        ready.append((half, spot))

    def multiply_one(half, spot, owner):
        columns = pl.ds(half * COLS, COLS)
        integrals[:, columns] += lax.dot_general(
            left_all[owner, spot], rights[half][owner, spot], (((0,), (0,)), ((), ())), preferred_element_type=F32
        )

    def multiply(limit, keep=2):
        for _ in range(limit):
            if len(ready) <= keep:
                return
            half, spot = ready.pop(0)

            def body(turn, carry):
                owner = (c + turn) % 2

                @pl.when(turn == 1)
                def _():
                    wait(rights[half].at[other, spot], core_recv.at[half, spot])

                multiply_one(half, spot, owner)
                return carry

            lax.fori_loop(0, 2, body, 0)

    for dz in (1, 3, 2):
        for half in range(2):
            exchange(dz, half)
    for half in range(2):
        rights[half][c, 0, 0:ROWS, :] = right_own[
            z // 2, :, pl.ds(pl.multiple_of((z % 2) * RIGHT + half * COLS, COLS), COLS)
        ]
        send_first(half, pl.ds(0, ROWS), 0)

    for step in range(1, PLANE):
        spot = (step * 5) % PLANE
        dy, dx = spot // RING, spot % RING
        block = ((y + dy) % RING) * RING + (x + dx) % RING
        remote(
            left_own.at[block // 8, :, pl.ds(pl.multiple_of((block % 8) * LEFT, LEFT), LEFT)],
            left.at[((-dy) % RING) * RING + (-dx) % RING, rows_of(0)],
            left_send,
            left_recv,
            device_of(y + dy, x + dx, z, c),
        )
    left[0, 0:ROWS, :] = left_own[own_block // 8, :, pl.ds(pl.multiple_of((own_block % 8) * LEFT, LEFT), LEFT)]

    middle, last = pl.ds(ROWS, 2 * ROWS), pl.ds(3 * ROWS, ROWS)
    for half in range(2):
        wait(rights[half].at[c, 0, middle], right_first.at[half, 0])
        send_first(half, middle, 0)
    for half in range(2):
        wait(rights[half].at[c, 0, last], right_first.at[half, 1])
        send_first(half, last, 1)
        share(half, 0)
    wait(left.at[pl.ds(0, PLANE - 1), rows_of(0)], left_recv)
    for sign in (1, -1):
        remote(
            left.at[:, rows_of(0)], left.at[:, rows_of(-sign)],
            spread_send, spread_recv.at[(-sign) % RING], device_of(y, x, z + sign, c),
        )
    integrals[...] = jnp.zeros_like(integrals)

    own_occ = occ[i_index[own_block // 8]] + occ[j_index[z // 2]]
    row_start = pl.multiple_of((own_block % 8) * LEFT + c * LEFT_CORE, LEFT_CORE)
    row = vir[:, pl.ds(row_start, LEFT_CORE)].astype(F32) - own_occ.astype(F32)
    vir_column[...] = jnp.transpose(jnp.broadcast_to(row, (128, LEFT_CORE)))

    for half in range(2):
        for sign in (1, -1):
            wait(rights[half].at[c, place(half, 0, (-sign) % RING), pl.ds(0, 3 * ROWS)],
                 right_recv.at[half, place(half, 0, (-sign) % RING), 0])
        relay_first(half, 1)
        send_second(half, 0)
    for sign in (1, -1):
        for half in range(2):
            wait(rights[half].at[c, place(half, 0, (-sign) % RING), last],
                 right_recv.at[half, place(half, 0, (-sign) % RING), 1])
            if sign == -1:
                relay_first(half, sign)
            send_second(half, (-sign) % RING)
            share(half, place(half, 0, (-sign) % RING))
    for sign in (1, -1):
        for half in range(2):
            arrived(half, (-sign) % RING, 0)
            relay_second(half, 0, sign)
            share(half, place(half, (-sign) % RING, 0))
    for sign in (1, -1):
        wait(left.at[:, rows_of(-sign)], spread_recv.at[(-sign) % RING])
        part = 0 if sign == 1 else 1
        spots = pl.ds(part * (PLANE // 2), PLANE // 2)
        remote(
            left.at[spots, rows_of(-sign)], left.at[spots, rows_of(2)],
            spread_send, spread_recv.at[2 * part], device_of(y, x, z + sign, c),
        )
    for half in range(2):
        arrived(half, 0, 2)
        send_second(half, 2)
        share(half, place(half, 0, 2))

    for part in range(2):
        wait(left.at[pl.ds(part * (PLANE // 2), PLANE // 2), rows_of(2)], spread_recv.at[2 * part])
    remote(
        left.at[:, :, pl.ds(pl.multiple_of(other * LEFT_CORE, LEFT_CORE), LEFT_CORE)], left_all.at[c],
        core_left.at[0], core_left.at[1], sibling,
    )
    mine = pltpu.make_async_copy(
        left.at[:, :, pl.ds(pl.multiple_of(c * LEFT_CORE, LEFT_CORE), LEFT_CORE)], left_all.at[c], core_left.at[2]
    )
    mine.start()
    for first in (3, 1):
        for sign in (1, -1):
            for half in range(2):
                arrived(half, (-sign) % RING, first)
                relay_second(half, first, sign)
                share(half, place(half, (-sign) % RING, first))
                if first == 3 and sign == 1 and half == 1:
                    mine.wait()
                    wait(left_all.at[other], core_left.at[1])
                if first == 1 or sign == -1:
                    multiply(2)
    for half in range(2):
        arrived(half, 2, 0)
        share(half, place(half, 2, 0))
        multiply(2)
    for sign in (1, -1):
        for half in range(2):
            arrived(half, (-sign) % RING, 2)
            relay_second(half, 2, sign)
            share(half, place(half, (-sign) % RING, 2))
            multiply(2)
    for first in (3, 1):
        for half in range(2):
            arrived(half, 2, first)
            share(half, place(half, 2, first))
            multiply(2)
    multiply(len(ready), 0)
    final = place(0, 2, 2)
    for half in range(2):
        arrived(half, 2, 2)
        share(half, final)
    for half in range(2):
        multiply_one(half, final, c)
    for half in range(2):
        wait(rights[half].at[other, final], core_recv.at[half, final])
        multiply_one(half, final, other)

        def divide(tile, carry):
            start = pl.multiple_of(half * COLS + tile * 128, 128)
            columns = pl.ds(start, 128)
            vir_row = vir[:, pl.ds(pl.multiple_of((z % 2) * RIGHT + start, 128), 128)].astype(F32)
            denominator = (vir_column[...] + vir_row) * (1.0 / 1024.0)
            amplitude[:, columns] = (integrals[:, columns] / denominator).astype(BF16)
            return carry

        lax.fori_loop(0, COLS // 128, divide, 0)

    def order(step):
        spot = step * 0
        for index, entry in enumerate(ORDER):
            spot = jnp.where(step == index, entry, spot)
        return spot

    def partial_rows(owner, dz):
        start = owner * PIECE + RANK[dz] * ROWS
        return slice(start, start + ROWS)

    def multiply_back(spot):
        total = None
        for half in range(2):
            term = lax.dot_general(
                rights[half][:, spot].reshape(2 * PIECE, COLS),
                amplitude[:, half * COLS : (half + 1) * COLS],
                (((1,), (1,)), ((), ())),
                preferred_element_type=F32,
            )
            total = term if total is None else total + term
        partial[spot] = total
        for way, dz in ((0, 1), (1, -1)):
            opposite[spot, way] = total[partial_rows(way, 2)].astype(BF16)
            remote(
                opposite.at[spot, way], relay.at[spot, way], opposite_send, relay_recv.at[spot],
                device_of(y, x, z + dz, c),
            )

    def pass_on(spot):
        wait(relay.at[spot], relay_recv.at[spot])
        for way, dz in ((0, 1), (1, -1)):
            for owner in range(2):
                total = partial[spot, partial_rows(owner, dz % RING), :]
                if owner == way:
                    total = total + relay[spot, way].astype(F32)
                ring_out[spot, way, owner] = total.astype(BF16)
            remote(
                ring_out.at[spot, way], ring_in.at[spot, way], ring_send, ring_recv.at[spot], device_of(y, x, z + dz, c)
            )

    own_columns = pl.ds(pl.multiple_of((own_block % 8) * LEFT + c * LEFT_CORE, LEFT_CORE), LEFT_CORE)
    own_target = gamma.at[own_block // 8, :, own_columns]

    def hand_over(spot):
        wait(ring_in.at[spot], ring_recv.at[spot])
        for owner in range(2):
            total_out[2 * spot + owner] = (
                partial[spot, partial_rows(owner, 0), :]
                + ring_in[spot, 0, owner].astype(F32)
                + ring_in[spot, 1, owner].astype(F32)
            )

    def back(step, carry):
        @pl.when(step < PLANE)
        def _():
            multiply_back(order(step))

        @pl.when((step >= LAG) & (step < PLANE + LAG))
        def _():
            pass_on(order(step - LAG))

        @pl.when(step >= 2 * LAG)
        def _():
            spot = order(step - 2 * LAG)
            hand_over(spot)

            @pl.when(step < PLANE + 2 * LAG - 1)
            def _():
                for owner in range(2):
                    remote(
                        total_out.at[2 * spot + owner], own_target, total_send, gamma_recv,
                        device_of(y + spot // RING, x + spot % RING, z, owner),
                    )

        return carry

    lax.fori_loop(0, PLANE + 2 * LAG, back, 0)
    remote(total_out.at[other], own_target, total_send, gamma_recv, sibling)
    keep = pltpu.make_async_copy(total_out.at[c], own_target, held_sem)
    keep.start()
    keep.wait()
    for sem in (gamma_recv, total_send):
        wait(total_out.at[pl.ds(0, 2 * PLANE - 1)], sem)

    wait(left.at[pl.ds(0, PLANE - 1), rows_of(0)], left_send)
    wait(left.at[:, pl.ds(0, PIECE - ROWS)], spread_send)
    wait(left_all.at[c], core_left.at[0])
    for half in range(2):
        wait(rights[half].at[c, 0, pl.ds(0, PIECE - ROWS)], right_send.at[half])
        wait(rights[half].at[c, pl.ds(0, PLANE - 1)], right_send.at[half])
        wait(rights[half].at[c], core_send.at[half])
    wait(opposite, opposite_send)
    wait(ring_out, ring_send)


def copy_kernel(source, target, held, sem):
    parts = [(n, pl.ds(row, 8), row // 8) for n in range(2) for row in range(0, ROWS, 8)]
    reads = [pltpu.make_async_copy(source.at[n, rows], held.at[n, rows], sem.at[0, n, k]) for n, rows, k in parts]
    writes = [pltpu.make_async_copy(held.at[n, rows], target.at[n, rows], sem.at[1, n, k]) for n, rows, k in parts]
    for read in reads:
        read.start()
    for read, write in zip(reads, writes):
        read.wait()
        write.start()
    for write in writes:
        write.wait()


def per_device(slabs, occ_energy, vir_energy, i_index, j_index):
    vmem = pl.BlockSpec(memory_space=pltpu.VMEM)
    anywhere = pl.BlockSpec(memory_space=pl.ANY)
    smem = pl.BlockSpec(memory_space=pltpu.SMEM)
    dma = pltpu.SemaphoreType.DMA
    gamma = pl.pallas_call(
        kernel,
        out_shape=jax.ShapeDtypeStruct((2, ROWS, NVIR), F32),
        in_specs=[anywhere, vmem, smem, smem, smem],
        out_specs=anywhere,
        scratch_shapes=[
            pltpu.VMEM((8, ROWS, NVIR), BF16),
            pltpu.VMEM((2, ROWS, NVIR), BF16),
            pltpu.VMEM((2, ROWS, NVIR), BF16),
            pltpu.VMEM((PLANE, PIECE, LEFT), BF16),
            pltpu.VMEM((2, PLANE, PIECE, LEFT_CORE), BF16),
            pltpu.VMEM((2, PLANE, PIECE, COLS), BF16),
            pltpu.VMEM((2, PLANE, PIECE, COLS), BF16),
            pltpu.VMEM((LEFT_CORE, RIGHT), F32),
            pltpu.VMEM((LEFT_CORE, RIGHT), BF16),
            pltpu.VMEM((LEFT_CORE, 128), F32),
            pltpu.VMEM((PLANE, 2 * PIECE, LEFT_CORE), F32),
            pltpu.VMEM((PLANE, 2, ROWS, LEFT_CORE), BF16),
            pltpu.VMEM((PLANE, 2, ROWS, LEFT_CORE), BF16),
            pltpu.VMEM((PLANE, 2, 2, ROWS, LEFT_CORE), BF16),
            pltpu.VMEM((PLANE, 2, 2, ROWS, LEFT_CORE), BF16),
            pltpu.VMEM((2 * PLANE, ROWS, LEFT_CORE), F32),
            dma, dma, dma, dma, dma((RING,)), dma((3,)), dma((2,)), dma((2, 2)), dma((2, PLANE, 2)),
            dma((2,)), dma((2, PLANE)), dma, dma((PLANE,)), dma, dma((PLANE,)), dma, dma,
        ],
        compiler_params=pltpu.CompilerParams(
            collective_id=0, has_side_effects=True, vmem_limit_bytes=60 * 2**20
        ),
        name="back_transform",
    )(slabs, vir_energy.reshape(1, NVIR), occ_energy, i_index, j_index)
    return pl.pallas_call(
        copy_kernel,
        out_shape=jax.ShapeDtypeStruct((2, ROWS, NVIR), F32),
        in_specs=[anywhere],
        out_specs=anywhere,
        scratch_shapes=[pltpu.VMEM((2, ROWS, NVIR), F32), dma((2, 2, ROWS // 8))],
        name="result",
    )(gamma)


def solution(mesh):
    placed = (P(None, ("aux", "pan"), None), P(), P(), P(), P())
    return jax.shard_map(
        per_device,
        mesh=mesh,
        in_specs=placed,
        out_specs=P(None, ("aux", "pan"), None),
        check_vma=False,
    )
```

```python
import jax
import jax.numpy as jnp
from jax import lax
from jax.experimental import pallas as pl
from jax.experimental.pallas import tpu as pltpu
from jax.sharding import PartitionSpec as P

MESH = pl.DeviceIdType.MESH
RING = 4
PLANE = RING * RING
ROWS = 48
NVIR = 4096
PIECE = RING * ROWS
HALF_PIECE = PIECE // 2
LEFT = 512
LEFT_CORE = LEFT // 2
RIGHT = 2048
COLS = RIGHT // 2
F32 = jnp.float32
BF16 = jnp.bfloat16
RELAY_LAG = 3
RING_LAG = 4
RANK = (0, 1, 3, 2)
ORDER = (10, 9, 11, 6, 14, 5, 15, 7, 13, 2, 8, 1, 3, 4, 12, 0)


def device_of(y, x, z, c):
    return ((y % RING) * 8 + (x % RING) * 2 + (z % RING) // 2, (z % 2) * 2 + c)


def rows_of(dz):
    return pl.ds(RANK[dz % RING] * ROWS, ROWS)


def kernel(
    slabs, vir, occ, i_index, j_index, gamma,
    held, left_own, right_own, left, left_all, right_a, right_b, integrals, amplitude, vir_column, inverse,
    partial, opposite, relay, ring_out, ring_in, total_out,
    held_sem, left_send, left_recv, spread_send, spread_recv, core_left, right_send, right_first, right_recv,
    core_send, core_recv, opposite_send, relay_recv, ring_send, ring_recv, total_send, gamma_recv,
):
    aux, pan = lax.axis_index("aux"), lax.axis_index("pan")
    y, x = aux // 8, (aux // 2) % RING
    z, c = (aux % 2) * 2 + pan // 2, pan % 2
    other = 1 - c
    sibling = device_of(y, x, z, other)
    rights = (right_a, right_b)
    own_block = y * RING + x

    def remote(src, dst, send, recv, to):
        copy = pltpu.make_async_remote_copy(
            src_ref=src, dst_ref=dst, send_sem=send, recv_sem=recv, device_id=to, device_id_type=MESH
        )
        copy.start()

    def wait(ref, sem):
        pltpu.make_async_copy(ref, ref, sem).wait()

    fetch = pltpu.make_async_copy(slabs, held, held_sem)
    fetch.start()
    barrier = pltpu.get_barrier_semaphore()

    def greet(to):
        pl.semaphore_signal(barrier, inc=1, device_id=to, device_id_type=MESH)

    for dz in range(1, RING):
        greet(device_of(y, x, z + dz, c))
    greet(sibling)
    for spot in range(1, PLANE):
        greet(device_of(y + spot // RING, x + spot % RING, z, c))
    fetch.wait()
    for slot in range(2):
        right_own[slot] = held[j_index[slot]]
    for slot in range(2):
        left_own[slot] = held[i_index[slot]]
    pl.semaphore_wait(barrier, RING - 1 + 1 + (PLANE - 1))

    def right_columns(to, half):
        return right_own.at[to // 2, :, pl.ds(pl.multiple_of((to % 2) * RIGHT + half * COLS, COLS), COLS)]

    def exchange(dz, half):
        remote(
            right_columns((z + dz) % RING, half), rights[half].at[c, 0, rows_of(-dz)], right_send.at[half],
            right_first.at[half, 1 if dz == 2 else 0], device_of(y, x, z + dz, c),
        )

    def place(half, second, first):
        return second * RING + first if half == 0 else first * RING + second

    def toward(half, second, first):
        return device_of(y + second, x + first, z, c) if half == 0 else device_of(y + first, x + second, z, c)

    def send_first(half, rows, part):
        for sign in (1, -1):
            spot = place(half, 0, (-sign) % RING)
            remote(
                rights[half].at[c, 0, rows], rights[half].at[c, spot, rows], right_send.at[half],
                right_recv.at[half, spot, part], toward(half, 0, sign),
            )

    def relay_first(half, sign):
        here, there = place(half, 0, (-sign) % RING), place(half, 0, 2)
        part = 0 if sign == 1 else 1
        rows = pl.ds(part * HALF_PIECE, HALF_PIECE)
        remote(
            rights[half].at[c, here, rows], rights[half].at[c, there, rows], right_send.at[half],
            right_recv.at[half, there, part], toward(half, 0, sign),
        )

    def send_second(half, first, rows=pl.ds(0, PIECE)):
        here = place(half, 0, first)
        for sign in (1, -1):
            there = place(half, (-sign) % RING, first)
            remote(
                rights[half].at[c, here, rows], rights[half].at[c, there, rows], right_send.at[half],
                right_recv.at[half, there, 0], toward(half, sign, 0),
            )

    def relay_second(half, first, sign):
        here, there = place(half, (-sign) % RING, first), place(half, 2, first)
        part = 0 if sign == 1 else 1
        rows = pl.ds(part * HALF_PIECE, HALF_PIECE)
        remote(
            rights[half].at[c, here, rows], rights[half].at[c, there, rows], right_send.at[half],
            right_recv.at[half, there, part], toward(half, sign, 0),
        )

    def arrived(half, second, first):
        spot = place(half, second, first)
        if second == 2 or (second == 0 and first == 2):
            for part in range(2):
                wait(rights[half].at[c, spot, pl.ds(part * HALF_PIECE, HALF_PIECE)], right_recv.at[half, spot, part])
        else:
            wait(rights[half].at[c, spot], right_recv.at[half, spot, 0])

    ready = []

    def share(half, spot):
        block = rights[half].at[c, spot]
        remote(block, block, core_send.at[half], core_recv.at[half, spot], sibling)
        ready.append((half, spot))

    def multiply_one(half, spot, owner):
        columns = pl.ds(half * COLS, COLS)
        integrals[:, columns] += lax.dot_general(
            left_all[owner, spot], rights[half][owner, spot], (((0,), (0,)), ((), ())), preferred_element_type=F32
        )

    def multiply(limit, keep=2):
        for _ in range(limit):
            if len(ready) <= keep:
                return
            half, spot = ready.pop(0)

            def body(turn, carry):
                owner = (c + turn) % 2

                @pl.when(turn == 1)
                def _():
                    wait(rights[half].at[other, spot], core_recv.at[half, spot])

                multiply_one(half, spot, owner)
                return carry

            lax.fori_loop(0, 2, body, 0)

    for dz in (1, 3, 2):
        for half in range(2):
            exchange(dz, half)
    for half in range(2):
        rights[half][c, 0, 0:ROWS, :] = right_own[
            z // 2, :, pl.ds(pl.multiple_of((z % 2) * RIGHT + half * COLS, COLS), COLS)
        ]
        send_first(half, pl.ds(0, ROWS), 0)

    for step in range(1, PLANE):
        spot = (step * 5) % PLANE
        dy, dx = spot // RING, spot % RING
        block = ((y + dy) % RING) * RING + (x + dx) % RING
        remote(
            left_own.at[block // 8, :, pl.ds(pl.multiple_of((block % 8) * LEFT, LEFT), LEFT)],
            left.at[((-dy) % RING) * RING + (-dx) % RING, rows_of(0)],
            left_send,
            left_recv,
            device_of(y + dy, x + dx, z, c),
        )
    left[0, 0:ROWS, :] = left_own[own_block // 8, :, pl.ds(pl.multiple_of((own_block % 8) * LEFT, LEFT), LEFT)]

    middle, last = pl.ds(ROWS, 2 * ROWS), pl.ds(3 * ROWS, ROWS)
    for half in range(2):
        wait(rights[half].at[c, 0, middle], right_first.at[half, 0])
        send_first(half, middle, 0)
    for half in range(2):
        wait(rights[half].at[c, 0, last], right_first.at[half, 1])
        send_first(half, last, 1)
        share(half, 0)
    wait(left.at[pl.ds(0, PLANE - 1), rows_of(0)], left_recv)
    for sign in (1, -1):
        remote(
            left.at[:, rows_of(0)], left.at[:, rows_of(-sign)],
            spread_send, spread_recv.at[(-sign) % RING], device_of(y, x, z + sign, c),
        )
    integrals[...] = jnp.zeros_like(integrals)

    own_occ = occ[i_index[own_block // 8]] + occ[j_index[z // 2]]
    row_start = pl.multiple_of((own_block % 8) * LEFT + c * LEFT_CORE, LEFT_CORE)
    row = vir[:, pl.ds(row_start, LEFT_CORE)].astype(F32) - own_occ.astype(F32)
    vir_column[...] = jnp.transpose(jnp.broadcast_to(row, (128, LEFT_CORE)))

    def invert(tile, carry):
        start = pl.multiple_of(tile * 128, 128)
        vir_row = vir[:, pl.ds(pl.multiple_of((z % 2) * RIGHT + start, 128), 128)].astype(F32)
        inverse[:, pl.ds(start, 128)] = 1.0 / ((vir_column[...] + vir_row) * (1.0 / 1024.0))
        return carry

    lax.fori_loop(0, RIGHT // 128, invert, 0)

    for half in range(2):
        for sign in (1, -1):
            wait(rights[half].at[c, place(half, 0, (-sign) % RING), pl.ds(0, 3 * ROWS)],
                 right_recv.at[half, place(half, 0, (-sign) % RING), 0])
        relay_first(half, 1)
        send_second(half, 0)
    for sign in (1, -1):
        for half in range(2):
            wait(rights[half].at[c, place(half, 0, (-sign) % RING), last],
                 right_recv.at[half, place(half, 0, (-sign) % RING), 1])
            if sign == -1:
                relay_first(half, sign)
            send_second(half, (-sign) % RING)
            share(half, place(half, 0, (-sign) % RING))
    for sign in (1, -1):
        for half in range(2):
            arrived(half, (-sign) % RING, 0)
            relay_second(half, 0, sign)
            share(half, place(half, (-sign) % RING, 0))
    for sign in (1, -1):
        wait(left.at[:, rows_of(-sign)], spread_recv.at[(-sign) % RING])
        part = 0 if sign == 1 else 1
        spots = pl.ds(part * (PLANE // 2), PLANE // 2)
        remote(
            left.at[spots, rows_of(-sign)], left.at[spots, rows_of(2)],
            spread_send, spread_recv.at[2 * part], device_of(y, x, z + sign, c),
        )
    for half in range(2):
        arrived(half, 0, 2)
        send_second(half, 2)
        share(half, place(half, 0, 2))

    for part in range(2):
        wait(left.at[pl.ds(part * (PLANE // 2), PLANE // 2), rows_of(2)], spread_recv.at[2 * part])
    remote(
        left.at[:, :, pl.ds(pl.multiple_of(other * LEFT_CORE, LEFT_CORE), LEFT_CORE)], left_all.at[c],
        core_left.at[0], core_left.at[1], sibling,
    )
    mine = pltpu.make_async_copy(
        left.at[:, :, pl.ds(pl.multiple_of(c * LEFT_CORE, LEFT_CORE), LEFT_CORE)], left_all.at[c], core_left.at[2]
    )
    mine.start()
    for first in (3, 1):
        for sign in (1, -1):
            for half in range(2):
                arrived(half, (-sign) % RING, first)
                relay_second(half, first, sign)
                share(half, place(half, (-sign) % RING, first))
                if first == 3 and sign == 1 and half == 1:
                    mine.wait()
                    wait(left_all.at[other], core_left.at[1])
                if first == 1 or sign == -1:
                    multiply(2)
    for half in range(2):
        arrived(half, 2, 0)
        share(half, place(half, 2, 0))
        multiply(2)
    for sign in (1, -1):
        for half in range(2):
            arrived(half, (-sign) % RING, 2)
            relay_second(half, 2, sign)
            share(half, place(half, (-sign) % RING, 2))
            multiply(2)
    for first in (3, 1):
        for half in range(2):
            arrived(half, 2, first)
            share(half, place(half, 2, first))
            multiply(2)
    multiply(len(ready), 0)
    final = place(0, 2, 2)
    for half in range(2):
        for part in range(2):
            block = rights[half].at[c, final, pl.ds(part * HALF_PIECE, HALF_PIECE)]
            wait(block, right_recv.at[half, final, part])
            remote(block, block, core_send.at[half], core_recv.at[half, final], sibling)
    for half in range(2):
        columns = pl.ds(half * COLS, COLS)
        wait(rights[half].at[other, final], core_recv.at[half, final])
        total = integrals[:, columns] + lax.dot_general(
            left_all[:, final].reshape(2 * PIECE, LEFT_CORE),
            rights[half][:, final].reshape(2 * PIECE, COLS),
            (((0,), (0,)), ((), ())),
            preferred_element_type=F32,
        )
        amplitude[:, columns] = (total * inverse[:, columns]).astype(BF16)

    def order(step):
        spot = step * 0
        for index, entry in enumerate(ORDER):
            spot = jnp.where(step == index, entry, spot)
        return spot

    def partial_rows(owner, dz):
        start = owner * PIECE + RANK[dz] * ROWS
        return slice(start, start + ROWS)

    def multiply_back(spot):
        total = None
        for half in range(2):
            term = lax.dot_general(
                rights[half][:, spot].reshape(2 * PIECE, COLS),
                amplitude[:, half * COLS : (half + 1) * COLS],
                (((1,), (1,)), ((), ())),
                preferred_element_type=F32,
            )
            total = term if total is None else total + term
        partial[spot] = total
        for way, dz in ((0, 1), (1, -1)):
            to = device_of(y, x, z + dz, c)
            opposite[spot, way] = total[partial_rows(way, 2)].astype(BF16)
            remote(opposite.at[spot, way], relay.at[spot, way], opposite_send, relay_recv.at[spot], to)
            straight = 1 - way
            ring_out[spot, way, straight] = total[partial_rows(straight, dz % RING)].astype(BF16)
            remote(
                ring_out.at[spot, way, straight], ring_in.at[spot, way, straight], ring_send, ring_recv.at[spot], to
            )

    def pass_on(spot):
        wait(relay.at[spot], relay_recv.at[spot])
        for way, dz in ((0, 1), (1, -1)):
            total = partial[spot, partial_rows(way, dz % RING), :] + relay[spot, way].astype(F32)
            ring_out[spot, way, way] = total.astype(BF16)
            remote(
                ring_out.at[spot, way, way], ring_in.at[spot, way, way], ring_send, ring_recv.at[spot],
                device_of(y, x, z + dz, c),
            )

    own_columns = pl.ds(pl.multiple_of((own_block % 8) * LEFT + c * LEFT_CORE, LEFT_CORE), LEFT_CORE)
    own_target = gamma.at[own_block // 8, :, own_columns]

    def hand_over(spot):
        wait(ring_in.at[spot], ring_recv.at[spot])
        for owner in range(2):
            total_out[2 * spot + owner] = (
                partial[spot, partial_rows(owner, 0), :]
                + ring_in[spot, 0, owner].astype(F32)
                + ring_in[spot, 1, owner].astype(F32)
            )

    def back(step, carry):
        @pl.when(step < PLANE)
        def _():
            multiply_back(order(step))

        @pl.when((step >= RELAY_LAG) & (step < PLANE + RELAY_LAG))
        def _():
            pass_on(order(step - RELAY_LAG))

        @pl.when(step >= RELAY_LAG + RING_LAG)
        def _():
            spot = order(step - RELAY_LAG - RING_LAG)
            hand_over(spot)

            @pl.when(step < PLANE + RELAY_LAG + RING_LAG - 1)
            def _():
                for owner in range(2):
                    remote(
                        total_out.at[2 * spot + owner], own_target, total_send, gamma_recv,
                        device_of(y + spot // RING, x + spot % RING, z, owner),
                    )

        return carry

    lax.fori_loop(0, PLANE + RELAY_LAG + RING_LAG, back, 0)
    remote(total_out.at[other], own_target, total_send, gamma_recv, sibling)
    keep = pltpu.make_async_copy(total_out.at[c], own_target, held_sem)
    keep.start()
    keep.wait()
    for sem in (gamma_recv, total_send):
        wait(total_out.at[pl.ds(0, 2 * PLANE - 1)], sem)

    wait(left.at[pl.ds(0, PLANE - 1), rows_of(0)], left_send)
    wait(left.at[:, pl.ds(0, PIECE - ROWS)], spread_send)
    wait(left_all.at[c], core_left.at[0])
    for half in range(2):
        wait(rights[half].at[c, 0, pl.ds(0, PIECE - ROWS)], right_send.at[half])
        wait(rights[half].at[c, pl.ds(0, PLANE - 1)], right_send.at[half])
        wait(rights[half].at[c], core_send.at[half])
    wait(opposite, opposite_send)
    wait(ring_out, ring_send)


def copy_kernel(source, target, held, sem):
    parts = [(n, pl.ds(row, 16), row // 16) for n in range(2) for row in range(0, ROWS, 16)]
    reads = [pltpu.make_async_copy(source.at[n, rows], held.at[n, rows], sem.at[0, n, k]) for n, rows, k in parts]
    writes = [pltpu.make_async_copy(held.at[n, rows], target.at[n, rows], sem.at[1, n, k]) for n, rows, k in parts]
    for read in reads:
        read.start()
    for read, write in zip(reads, writes):
        read.wait()
        write.start()
    for write in writes:
        write.wait()


def per_device(slabs, occ_energy, vir_energy, i_index, j_index):
    vmem = pl.BlockSpec(memory_space=pltpu.VMEM)
    anywhere = pl.BlockSpec(memory_space=pl.ANY)
    smem = pl.BlockSpec(memory_space=pltpu.SMEM)
    dma = pltpu.SemaphoreType.DMA
    gamma = pl.pallas_call(
        kernel,
        out_shape=jax.ShapeDtypeStruct((2, ROWS, NVIR), F32),
        in_specs=[anywhere, vmem, smem, smem, smem],
        out_specs=anywhere,
        scratch_shapes=[
            pltpu.VMEM((8, ROWS, NVIR), BF16),
            pltpu.VMEM((2, ROWS, NVIR), BF16),
            pltpu.VMEM((2, ROWS, NVIR), BF16),
            pltpu.VMEM((PLANE, PIECE, LEFT), BF16),
            pltpu.VMEM((2, PLANE, PIECE, LEFT_CORE), BF16),
            pltpu.VMEM((2, PLANE, PIECE, COLS), BF16),
            pltpu.VMEM((2, PLANE, PIECE, COLS), BF16),
            pltpu.VMEM((LEFT_CORE, RIGHT), F32),
            pltpu.VMEM((LEFT_CORE, RIGHT), BF16),
            pltpu.VMEM((LEFT_CORE, 128), F32),
            pltpu.VMEM((LEFT_CORE, RIGHT), F32),
            pltpu.VMEM((PLANE, 2 * PIECE, LEFT_CORE), F32),
            pltpu.VMEM((PLANE, 2, ROWS, LEFT_CORE), BF16),
            pltpu.VMEM((PLANE, 2, ROWS, LEFT_CORE), BF16),
            pltpu.VMEM((PLANE, 2, 2, ROWS, LEFT_CORE), BF16),
            pltpu.VMEM((PLANE, 2, 2, ROWS, LEFT_CORE), BF16),
            pltpu.VMEM((2 * PLANE, ROWS, LEFT_CORE), F32),
            dma, dma, dma, dma, dma((RING,)), dma((3,)), dma((2,)), dma((2, 2)), dma((2, PLANE, 2)),
            dma((2,)), dma((2, PLANE)), dma, dma((PLANE,)), dma, dma((PLANE,)), dma, dma,
        ],
        compiler_params=pltpu.CompilerParams(
            collective_id=0, has_side_effects=True, vmem_limit_bytes=60 * 2**20
        ),
        name="back_transform",
    )(slabs, vir_energy.reshape(1, NVIR), occ_energy, i_index, j_index)
    return pl.pallas_call(
        copy_kernel,
        out_shape=jax.ShapeDtypeStruct((2, ROWS, NVIR), F32),
        in_specs=[anywhere],
        out_specs=anywhere,
        scratch_shapes=[pltpu.VMEM((2, ROWS, NVIR), F32), dma((2, 2, ROWS // 16))],
        name="result",
    )(gamma)


def solution(mesh):
    placed = (P(None, ("aux", "pan"), None), P(), P(), P(), P())
    return jax.shard_map(
        per_device,
        mesh=mesh,
        in_specs=placed,
        out_specs=P(None, ("aux", "pan"), None),
        check_vma=False,
    )
```

```python
import jax
import jax.numpy as jnp
from jax import lax
from jax.experimental import pallas as pl
from jax.experimental.pallas import tpu as pltpu
from jax.sharding import PartitionSpec as P

MESH = pl.DeviceIdType.MESH
RING = 4
PLANE = RING * RING
ROWS = 48
NVIR = 4096
PIECE = RING * ROWS
HALF_PIECE = PIECE // 2
LEFT = 512
LEFT_CORE = LEFT // 2
RIGHT = 2048
COLS = RIGHT // 2
F32 = jnp.float32
BF16 = jnp.bfloat16
RELAY_LAG = 3
RING_LAG = 4
RANK = (0, 1, 3, 2)
ORDER = (10, 9, 11, 6, 14, 5, 15, 7, 13, 2, 8, 1, 3, 4, 12, 0)


def device_of(y, x, z, c):
    return ((y % RING) * 8 + (x % RING) * 2 + (z % RING) // 2, (z % 2) * 2 + c)


def rows_of(dz):
    return pl.ds(RANK[dz % RING] * ROWS, ROWS)


def kernel(
    slabs, vir_in, occ_in, i_in, j_in, gamma,
    held, vir, occ, i_index, j_index, left_own, right_own, left, left_all, right_a, right_b, integrals, amplitude, vir_column, inverse,
    partial, opposite, relay, ring_out, ring_in, total_out,
    held_sem, fetch_sem, left_send, left_recv, spread_send, spread_recv, core_left, right_send, right_first, right_recv,
    core_send, core_recv, opposite_send, relay_recv, ring_send, ring_recv, total_send, gamma_recv,
):
    aux, pan = lax.axis_index("aux"), lax.axis_index("pan")
    y, x = aux // 8, (aux // 2) % RING
    z, c = (aux % 2) * 2 + pan // 2, pan % 2
    other = 1 - c
    sibling = device_of(y, x, z, other)
    rights = (right_a, right_b)
    own_block = y * RING + x

    def remote(src, dst, send, recv, to):
        copy = pltpu.make_async_remote_copy(
            src_ref=src, dst_ref=dst, send_sem=send, recv_sem=recv, device_id=to, device_id_type=MESH
        )
        copy.start()

    def wait(ref, sem):
        pltpu.make_async_copy(ref, ref, sem).wait()

    fetches = [
        pltpu.make_async_copy(source, target, fetch_sem.at[index])
        for index, (source, target) in enumerate(
            ((j_in, j_index), (i_in, i_index), (occ_in, occ), (vir_in, vir), (slabs, held))
        )
    ]
    for fetch in fetches:
        fetch.start()
    barrier = pltpu.get_barrier_semaphore()

    def greet(to):
        pl.semaphore_signal(barrier, inc=1, device_id=to, device_id_type=MESH)

    for dz in range(1, RING):
        greet(device_of(y, x, z + dz, c))
    greet(sibling)
    for spot in range(1, PLANE):
        greet(device_of(y + spot // RING, x + spot % RING, z, c))
    for fetch in fetches:
        fetch.wait()
    for slot in range(2):
        right_own[slot] = held[j_index[slot]]
    for slot in range(2):
        left_own[slot] = held[i_index[slot]]
    pl.semaphore_wait(barrier, RING - 1 + 1 + (PLANE - 1))

    def right_columns(to, half):
        return right_own.at[to // 2, :, pl.ds(pl.multiple_of((to % 2) * RIGHT + half * COLS, COLS), COLS)]

    def exchange(dz, half):
        remote(
            right_columns((z + dz) % RING, half), rights[half].at[c, 0, rows_of(-dz)], right_send.at[half],
            right_first.at[half, 1 if dz == 2 else 0], device_of(y, x, z + dz, c),
        )

    def place(half, second, first):
        return second * RING + first if half == 0 else first * RING + second

    def toward(half, second, first):
        return device_of(y + second, x + first, z, c) if half == 0 else device_of(y + first, x + second, z, c)

    def send_first(half, rows, part):
        for sign in (1, -1):
            spot = place(half, 0, (-sign) % RING)
            remote(
                rights[half].at[c, 0, rows], rights[half].at[c, spot, rows], right_send.at[half],
                right_recv.at[half, spot, part], toward(half, 0, sign),
            )

    def relay_first(half, sign):
        here, there = place(half, 0, (-sign) % RING), place(half, 0, 2)
        part = 0 if sign == 1 else 1
        rows = pl.ds(part * HALF_PIECE, HALF_PIECE)
        remote(
            rights[half].at[c, here, rows], rights[half].at[c, there, rows], right_send.at[half],
            right_recv.at[half, there, part], toward(half, 0, sign),
        )

    def send_second(half, first, rows=pl.ds(0, PIECE)):
        here = place(half, 0, first)
        for sign in (1, -1):
            there = place(half, (-sign) % RING, first)
            remote(
                rights[half].at[c, here, rows], rights[half].at[c, there, rows], right_send.at[half],
                right_recv.at[half, there, 0], toward(half, sign, 0),
            )

    def relay_second(half, first, sign):
        here, there = place(half, (-sign) % RING, first), place(half, 2, first)
        part = 0 if sign == 1 else 1
        rows = pl.ds(part * HALF_PIECE, HALF_PIECE)
        remote(
            rights[half].at[c, here, rows], rights[half].at[c, there, rows], right_send.at[half],
            right_recv.at[half, there, part], toward(half, sign, 0),
        )

    def arrived(half, second, first):
        spot = place(half, second, first)
        if second == 2 or (second == 0 and first == 2):
            for part in range(2):
                wait(rights[half].at[c, spot, pl.ds(part * HALF_PIECE, HALF_PIECE)], right_recv.at[half, spot, part])
        else:
            wait(rights[half].at[c, spot], right_recv.at[half, spot, 0])

    ready = []

    def share(half, spot):
        block = rights[half].at[c, spot]
        remote(block, block, core_send.at[half], core_recv.at[half, spot], sibling)
        ready.append((half, spot))

    def multiply_one(half, spot, owner):
        columns = pl.ds(half * COLS, COLS)
        integrals[:, columns] += lax.dot_general(
            left_all[owner, spot], rights[half][owner, spot], (((0,), (0,)), ((), ())), preferred_element_type=F32
        )

    def multiply(limit, keep=2):
        for _ in range(limit):
            if len(ready) <= keep:
                return
            half, spot = ready.pop(0)

            def body(turn, carry):
                owner = (c + turn) % 2

                @pl.when(turn == 1)
                def _():
                    wait(rights[half].at[other, spot], core_recv.at[half, spot])

                multiply_one(half, spot, owner)
                return carry

            lax.fori_loop(0, 2, body, 0)

    for dz in (1, 3, 2):
        for half in range(2):
            exchange(dz, half)
    for half in range(2):
        rights[half][c, 0, 0:ROWS, :] = right_own[
            z // 2, :, pl.ds(pl.multiple_of((z % 2) * RIGHT + half * COLS, COLS), COLS)
        ]
        send_first(half, pl.ds(0, ROWS), 0)

    for step in range(1, PLANE):
        spot = (step * 5) % PLANE
        dy, dx = spot // RING, spot % RING
        block = ((y + dy) % RING) * RING + (x + dx) % RING
        remote(
            left_own.at[block // 8, :, pl.ds(pl.multiple_of((block % 8) * LEFT, LEFT), LEFT)],
            left.at[((-dy) % RING) * RING + (-dx) % RING, rows_of(0)],
            left_send,
            left_recv,
            device_of(y + dy, x + dx, z, c),
        )
    left[0, 0:ROWS, :] = left_own[own_block // 8, :, pl.ds(pl.multiple_of((own_block % 8) * LEFT, LEFT), LEFT)]

    middle, last = pl.ds(ROWS, 2 * ROWS), pl.ds(3 * ROWS, ROWS)
    for half in range(2):
        wait(rights[half].at[c, 0, middle], right_first.at[half, 0])
        send_first(half, middle, 0)
    for half in range(2):
        wait(rights[half].at[c, 0, last], right_first.at[half, 1])
        send_first(half, last, 1)
        share(half, 0)
    wait(left.at[pl.ds(0, PLANE - 1), rows_of(0)], left_recv)
    for sign in (1, -1):
        remote(
            left.at[:, rows_of(0)], left.at[:, rows_of(-sign)],
            spread_send, spread_recv.at[(-sign) % RING], device_of(y, x, z + sign, c),
        )
    integrals[...] = jnp.zeros_like(integrals)

    own_occ = occ[i_index[own_block // 8]] + occ[j_index[z // 2]]
    row_start = pl.multiple_of((own_block % 8) * LEFT + c * LEFT_CORE, LEFT_CORE)
    row = vir[:, pl.ds(row_start, LEFT_CORE)].astype(F32) - own_occ.astype(F32)
    vir_column[...] = jnp.transpose(jnp.broadcast_to(row, (128, LEFT_CORE)))

    def invert(tile, carry):
        start = pl.multiple_of(tile * 128, 128)
        vir_row = vir[:, pl.ds(pl.multiple_of((z % 2) * RIGHT + start, 128), 128)].astype(F32)
        inverse[:, pl.ds(start, 128)] = 1.0 / ((vir_column[...] + vir_row) * (1.0 / 1024.0))
        return carry

    lax.fori_loop(0, RIGHT // 128, invert, 0)

    for half in range(2):
        for sign in (1, -1):
            wait(rights[half].at[c, place(half, 0, (-sign) % RING), pl.ds(0, 3 * ROWS)],
                 right_recv.at[half, place(half, 0, (-sign) % RING), 0])
        relay_first(half, 1)
        send_second(half, 0)
    for sign in (1, -1):
        for half in range(2):
            wait(rights[half].at[c, place(half, 0, (-sign) % RING), last],
                 right_recv.at[half, place(half, 0, (-sign) % RING), 1])
            if sign == -1:
                relay_first(half, sign)
            send_second(half, (-sign) % RING)
            share(half, place(half, 0, (-sign) % RING))
    for sign in (1, -1):
        for half in range(2):
            arrived(half, (-sign) % RING, 0)
            relay_second(half, 0, sign)
            share(half, place(half, (-sign) % RING, 0))
    for sign in (1, -1):
        wait(left.at[:, rows_of(-sign)], spread_recv.at[(-sign) % RING])
        part = 0 if sign == 1 else 1
        spots = pl.ds(part * (PLANE // 2), PLANE // 2)
        remote(
            left.at[spots, rows_of(-sign)], left.at[spots, rows_of(2)],
            spread_send, spread_recv.at[2 * part], device_of(y, x, z + sign, c),
        )
    for half in range(2):
        arrived(half, 0, 2)
        send_second(half, 2)
        share(half, place(half, 0, 2))

    for part in range(2):
        wait(left.at[pl.ds(part * (PLANE // 2), PLANE // 2), rows_of(2)], spread_recv.at[2 * part])
    remote(
        left.at[:, :, pl.ds(pl.multiple_of(other * LEFT_CORE, LEFT_CORE), LEFT_CORE)], left_all.at[c],
        core_left.at[0], core_left.at[1], sibling,
    )
    mine = pltpu.make_async_copy(
        left.at[:, :, pl.ds(pl.multiple_of(c * LEFT_CORE, LEFT_CORE), LEFT_CORE)], left_all.at[c], core_left.at[2]
    )
    mine.start()
    for first in (3, 1):
        for sign in (1, -1):
            for half in range(2):
                arrived(half, (-sign) % RING, first)
                relay_second(half, first, sign)
                share(half, place(half, (-sign) % RING, first))
                if first == 3 and sign == 1 and half == 1:
                    mine.wait()
                    wait(left_all.at[other], core_left.at[1])
                if first == 1 or sign == -1:
                    multiply(2)
    for half in range(2):
        arrived(half, 2, 0)
        share(half, place(half, 2, 0))
        multiply(2)
    for sign in (1, -1):
        for half in range(2):
            arrived(half, (-sign) % RING, 2)
            relay_second(half, 2, sign)
            share(half, place(half, (-sign) % RING, 2))
            multiply(2)
    for first in (3, 1):
        for half in range(2):
            arrived(half, 2, first)
            share(half, place(half, 2, first))
            multiply(2)
    multiply(len(ready), 0)
    final = place(0, 2, 2)
    for half in range(2):
        for part in range(2):
            block = rights[half].at[c, final, pl.ds(part * HALF_PIECE, HALF_PIECE)]
            wait(block, right_recv.at[half, final, part])
            remote(block, block, core_send.at[half], core_recv.at[half, final], sibling)
    for half in range(2):
        columns = pl.ds(half * COLS, COLS)
        wait(rights[half].at[other, final], core_recv.at[half, final])
        total = integrals[:, columns] + lax.dot_general(
            left_all[:, final].reshape(2 * PIECE, LEFT_CORE),
            rights[half][:, final].reshape(2 * PIECE, COLS),
            (((0,), (0,)), ((), ())),
            preferred_element_type=F32,
        )
        amplitude[:, columns] = (total * inverse[:, columns]).astype(BF16)

    def order(step):
        spot = step * 0
        for index, entry in enumerate(ORDER):
            spot = jnp.where(step == index, entry, spot)
        return spot

    def partial_rows(owner, dz):
        start = owner * PIECE + RANK[dz] * ROWS
        return slice(start, start + ROWS)

    def multiply_back(spot):
        total = None
        for half in range(2):
            term = lax.dot_general(
                rights[half][:, spot].reshape(2 * PIECE, COLS),
                amplitude[:, half * COLS : (half + 1) * COLS],
                (((1,), (1,)), ((), ())),
                preferred_element_type=F32,
            )
            total = term if total is None else total + term
        partial[spot] = total
        for way, dz in ((0, 1), (1, -1)):
            to = device_of(y, x, z + dz, c)
            opposite[spot, way] = total[partial_rows(way, 2)].astype(BF16)
            remote(opposite.at[spot, way], relay.at[spot, way], opposite_send, relay_recv.at[spot], to)
            straight = 1 - way
            ring_out[spot, way, straight] = total[partial_rows(straight, dz % RING)].astype(BF16)
            remote(
                ring_out.at[spot, way, straight], ring_in.at[spot, way, straight], ring_send, ring_recv.at[spot], to
            )

    def pass_on(spot):
        wait(relay.at[spot], relay_recv.at[spot])
        for way, dz in ((0, 1), (1, -1)):
            total = partial[spot, partial_rows(way, dz % RING), :] + relay[spot, way].astype(F32)
            ring_out[spot, way, way] = total.astype(BF16)
            remote(
                ring_out.at[spot, way, way], ring_in.at[spot, way, way], ring_send, ring_recv.at[spot],
                device_of(y, x, z + dz, c),
            )

    own_columns = pl.ds(pl.multiple_of((own_block % 8) * LEFT + c * LEFT_CORE, LEFT_CORE), LEFT_CORE)
    own_target = gamma.at[own_block // 8, :, own_columns]

    def hand_over(spot):
        wait(ring_in.at[spot], ring_recv.at[spot])
        for owner in range(2):
            total_out[2 * spot + owner] = (
                partial[spot, partial_rows(owner, 0), :]
                + ring_in[spot, 0, owner].astype(F32)
                + ring_in[spot, 1, owner].astype(F32)
            )

    def back(step, carry):
        @pl.when(step < PLANE)
        def _():
            multiply_back(order(step))

        @pl.when((step >= RELAY_LAG) & (step < PLANE + RELAY_LAG))
        def _():
            pass_on(order(step - RELAY_LAG))

        @pl.when(step >= RELAY_LAG + RING_LAG)
        def _():
            spot = order(step - RELAY_LAG - RING_LAG)
            hand_over(spot)

            @pl.when(step < PLANE + RELAY_LAG + RING_LAG - 1)
            def _():
                for owner in range(2):
                    remote(
                        total_out.at[2 * spot + owner], own_target, total_send, gamma_recv,
                        device_of(y + spot // RING, x + spot % RING, z, owner),
                    )

        return carry

    lax.fori_loop(0, PLANE + RELAY_LAG + RING_LAG, back, 0)
    remote(total_out.at[other], own_target, total_send, gamma_recv, sibling)
    keep = pltpu.make_async_copy(total_out.at[c], own_target, held_sem)
    keep.start()
    keep.wait()
    for sem in (gamma_recv, total_send):
        wait(total_out.at[pl.ds(0, 2 * PLANE - 1)], sem)

    wait(left.at[pl.ds(0, PLANE - 1), rows_of(0)], left_send)
    wait(left.at[:, pl.ds(0, PIECE - ROWS)], spread_send)
    wait(left_all.at[c], core_left.at[0])
    for half in range(2):
        wait(rights[half].at[c, 0, pl.ds(0, PIECE - ROWS)], right_send.at[half])
        wait(rights[half].at[c, pl.ds(0, PLANE - 1)], right_send.at[half])
        wait(rights[half].at[c], core_send.at[half])
    wait(opposite, opposite_send)
    wait(ring_out, ring_send)


def copy_kernel(source, target, held, sem):
    parts = [(n, pl.ds(row, 16), row // 16) for n in range(2) for row in range(0, ROWS, 16)]
    reads = [pltpu.make_async_copy(source.at[n, rows], held.at[n, rows], sem.at[0, n, k]) for n, rows, k in parts]
    writes = [pltpu.make_async_copy(held.at[n, rows], target.at[n, rows], sem.at[1, n, k]) for n, rows, k in parts]
    for read in reads:
        read.start()
    for read, write in zip(reads, writes):
        read.wait()
        write.start()
    for write in writes:
        write.wait()


def per_device(slabs, occ_energy, vir_energy, i_index, j_index):
    anywhere = pl.BlockSpec(memory_space=pl.ANY)
    dma = pltpu.SemaphoreType.DMA
    gamma = pl.pallas_call(
        kernel,
        out_shape=jax.ShapeDtypeStruct((2, ROWS, NVIR), F32),
        in_specs=[anywhere] * 5,
        out_specs=anywhere,
        scratch_shapes=[
            pltpu.VMEM((8, ROWS, NVIR), BF16),
            pltpu.VMEM((1, NVIR), jnp.int32),
            pltpu.SMEM((8,), jnp.int32),
            pltpu.SMEM((2,), jnp.int32),
            pltpu.SMEM((2,), jnp.int32),
            pltpu.VMEM((2, ROWS, NVIR), BF16),
            pltpu.VMEM((2, ROWS, NVIR), BF16),
            pltpu.VMEM((PLANE, PIECE, LEFT), BF16),
            pltpu.VMEM((2, PLANE, PIECE, LEFT_CORE), BF16),
            pltpu.VMEM((2, PLANE, PIECE, COLS), BF16),
            pltpu.VMEM((2, PLANE, PIECE, COLS), BF16),
            pltpu.VMEM((LEFT_CORE, RIGHT), F32),
            pltpu.VMEM((LEFT_CORE, RIGHT), BF16),
            pltpu.VMEM((LEFT_CORE, 128), F32),
            pltpu.VMEM((LEFT_CORE, RIGHT), F32),
            pltpu.VMEM((PLANE, 2 * PIECE, LEFT_CORE), F32),
            pltpu.VMEM((PLANE, 2, ROWS, LEFT_CORE), BF16),
            pltpu.VMEM((PLANE, 2, ROWS, LEFT_CORE), BF16),
            pltpu.VMEM((PLANE, 2, 2, ROWS, LEFT_CORE), BF16),
            pltpu.VMEM((PLANE, 2, 2, ROWS, LEFT_CORE), BF16),
            pltpu.VMEM((2 * PLANE, ROWS, LEFT_CORE), F32),
            dma, dma((5,)), dma, dma, dma, dma((RING,)), dma((3,)), dma((2,)), dma((2, 2)), dma((2, PLANE, 2)),
            dma((2,)), dma((2, PLANE)), dma, dma((PLANE,)), dma, dma((PLANE,)), dma, dma,
        ],
        compiler_params=pltpu.CompilerParams(
            collective_id=0, has_side_effects=True, vmem_limit_bytes=60 * 2**20
        ),
        name="back_transform",
    )(slabs, vir_energy.reshape(1, NVIR), occ_energy, i_index, j_index)
    return pl.pallas_call(
        copy_kernel,
        out_shape=jax.ShapeDtypeStruct((2, ROWS, NVIR), F32),
        in_specs=[anywhere],
        out_specs=anywhere,
        scratch_shapes=[pltpu.VMEM((2, ROWS, NVIR), F32), dma((2, 2, ROWS // 16))],
        name="result",
    )(gamma)


def solution(mesh):
    placed = (P(None, ("aux", "pan"), None), P(), P(), P(), P())
    return jax.shard_map(
        per_device,
        mesh=mesh,
        in_specs=placed,
        out_specs=P(None, ("aux", "pan"), None),
        check_vma=False,
    )
```

```python
import jax
import jax.numpy as jnp
from jax import lax
from jax.experimental import pallas as pl
from jax.experimental.pallas import tpu as pltpu
from jax.sharding import PartitionSpec as P

MESH = pl.DeviceIdType.MESH
RING = 4
PLANE = RING * RING
ROWS = 48
NVIR = 4096
PIECE = RING * ROWS
HALF_PIECE = PIECE // 2
LEFT = 512
LEFT_CORE = LEFT // 2
RIGHT = 2048
COLS = RIGHT // 2
F32 = jnp.float32
BF16 = jnp.bfloat16
RELAY_LAG = 4
RING_LAG = 4
RANK = (0, 1, 3, 2)
ORDER = (10, 9, 11, 6, 14, 5, 15, 7, 13, 2, 8, 1, 3, 4, 12, 0)


def device_of(y, x, z, c):
    return ((y % RING) * 8 + (x % RING) * 2 + (z % RING) // 2, (z % 2) * 2 + c)


def rows_of(dz):
    return pl.ds(RANK[dz % RING] * ROWS, ROWS)


def kernel(
    slabs, vir_in, occ_in, i_in, j_in, gamma,
    held, vir, occ, i_index, j_index, left_own, right_own, left, left_all, right_a, right_b, integrals, amplitude, vir_column, inverse,
    partial, opposite, relay, ring_out, ring_in, total_out,
    held_sem, fetch_sem, left_send, left_recv, spread_send, spread_recv, core_left, right_send, right_first, right_recv,
    core_send, core_recv, opposite_send, relay_recv, ring_send, ring_recv, total_send, gamma_recv,
):
    aux, pan = lax.axis_index("aux"), lax.axis_index("pan")
    y, x = aux // 8, (aux // 2) % RING
    z, c = (aux % 2) * 2 + pan // 2, pan % 2
    other = 1 - c
    sibling = device_of(y, x, z, other)
    rights = (right_a, right_b)
    own_block = y * RING + x

    def remote(src, dst, send, recv, to):
        copy = pltpu.make_async_remote_copy(
            src_ref=src, dst_ref=dst, send_sem=send, recv_sem=recv, device_id=to, device_id_type=MESH
        )
        copy.start()

    def wait(ref, sem):
        pltpu.make_async_copy(ref, ref, sem).wait()

    fetches = [
        pltpu.make_async_copy(source, target, fetch_sem.at[index])
        for index, (source, target) in enumerate(
            ((j_in, j_index), (i_in, i_index), (occ_in, occ), (vir_in, vir), (slabs, held))
        )
    ]
    for fetch in fetches:
        fetch.start()
    barrier = pltpu.get_barrier_semaphore()

    def greet(to):
        pl.semaphore_signal(barrier, inc=1, device_id=to, device_id_type=MESH)

    for dz in range(1, RING):
        greet(device_of(y, x, z + dz, c))
    greet(sibling)
    for spot in range(1, PLANE):
        greet(device_of(y + spot // RING, x + spot % RING, z, c))
    for fetch in fetches:
        fetch.wait()
    for slot in range(2):
        right_own[slot] = held[j_index[slot]]
    for slot in range(2):
        left_own[slot] = held[i_index[slot]]
    pl.semaphore_wait(barrier, RING - 1 + 1 + (PLANE - 1))

    def right_columns(to, half):
        return right_own.at[to // 2, :, pl.ds(pl.multiple_of((to % 2) * RIGHT + half * COLS, COLS), COLS)]

    def exchange(dz, half):
        remote(
            right_columns((z + dz) % RING, half), rights[half].at[c, 0, rows_of(-dz)], right_send.at[half],
            right_first.at[half, 1 if dz == 2 else 0], device_of(y, x, z + dz, c),
        )

    def place(half, second, first):
        return second * RING + first if half == 0 else first * RING + second

    def toward(half, second, first):
        return device_of(y + second, x + first, z, c) if half == 0 else device_of(y + first, x + second, z, c)

    def send_first(half, rows, part):
        for sign in (1, -1):
            spot = place(half, 0, (-sign) % RING)
            remote(
                rights[half].at[c, 0, rows], rights[half].at[c, spot, rows], right_send.at[half],
                right_recv.at[half, spot, part], toward(half, 0, sign),
            )

    def relay_first(half, sign):
        here, there = place(half, 0, (-sign) % RING), place(half, 0, 2)
        part = 0 if sign == 1 else 1
        rows = pl.ds(part * HALF_PIECE, HALF_PIECE)
        remote(
            rights[half].at[c, here, rows], rights[half].at[c, there, rows], right_send.at[half],
            right_recv.at[half, there, part], toward(half, 0, sign),
        )

    def send_second(half, first, rows=pl.ds(0, PIECE)):
        here = place(half, 0, first)
        for sign in (1, -1):
            there = place(half, (-sign) % RING, first)
            remote(
                rights[half].at[c, here, rows], rights[half].at[c, there, rows], right_send.at[half],
                right_recv.at[half, there, 0], toward(half, sign, 0),
            )

    def relay_second(half, first, sign):
        here, there = place(half, (-sign) % RING, first), place(half, 2, first)
        part = 0 if sign == 1 else 1
        rows = pl.ds(part * HALF_PIECE, HALF_PIECE)
        remote(
            rights[half].at[c, here, rows], rights[half].at[c, there, rows], right_send.at[half],
            right_recv.at[half, there, part], toward(half, sign, 0),
        )

    def arrived(half, second, first):
        spot = place(half, second, first)
        if second == 2 or (second == 0 and first == 2):
            for part in range(2):
                wait(rights[half].at[c, spot, pl.ds(part * HALF_PIECE, HALF_PIECE)], right_recv.at[half, spot, part])
        else:
            wait(rights[half].at[c, spot], right_recv.at[half, spot, 0])

    ready = []

    def share(half, spot):
        block = rights[half].at[c, spot]
        remote(block, block, core_send.at[half], core_recv.at[half, spot], sibling)
        ready.append((half, spot))

    def multiply_one(half, spot, owner):
        columns = pl.ds(half * COLS, COLS)
        integrals[:, columns] += lax.dot_general(
            left_all[owner, spot], rights[half][owner, spot], (((0,), (0,)), ((), ())), preferred_element_type=F32
        )

    def multiply(limit, keep=2):
        for _ in range(limit):
            if len(ready) <= keep:
                return
            half, spot = ready.pop(0)

            def body(turn, carry):
                owner = (c + turn) % 2

                @pl.when(turn == 1)
                def _():
                    wait(rights[half].at[other, spot], core_recv.at[half, spot])

                multiply_one(half, spot, owner)
                return carry

            lax.fori_loop(0, 2, body, 0)

    for dz in (1, 3, 2):
        for half in range(2):
            exchange(dz, half)
    for step in range(1, PLANE):
        spot = (step * 5) % PLANE
        dy, dx = spot // RING, spot % RING
        block = ((y + dy) % RING) * RING + (x + dx) % RING
        remote(
            left_own.at[block // 8, :, pl.ds(pl.multiple_of((block % 8) * LEFT, LEFT), LEFT)],
            left.at[((-dy) % RING) * RING + (-dx) % RING, rows_of(0)],
            left_send,
            left_recv,
            device_of(y + dy, x + dx, z, c),
        )
    left[0, 0:ROWS, :] = left_own[own_block // 8, :, pl.ds(pl.multiple_of((own_block % 8) * LEFT, LEFT), LEFT)]

    for half in range(2):
        rights[half][c, 0, 0:ROWS, :] = right_own[
            z // 2, :, pl.ds(pl.multiple_of((z % 2) * RIGHT + half * COLS, COLS), COLS)
        ]
        send_first(half, pl.ds(0, ROWS), 0)

    middle, last = pl.ds(ROWS, 2 * ROWS), pl.ds(3 * ROWS, ROWS)
    for half in range(2):
        wait(rights[half].at[c, 0, middle], right_first.at[half, 0])
        send_first(half, middle, 0)
    for half in range(2):
        wait(rights[half].at[c, 0, last], right_first.at[half, 1])
        send_first(half, last, 1)
        share(half, 0)
    wait(left.at[pl.ds(0, PLANE - 1), rows_of(0)], left_recv)
    for sign in (1, -1):
        remote(
            left.at[:, rows_of(0)], left.at[:, rows_of(-sign)],
            spread_send, spread_recv.at[(-sign) % RING], device_of(y, x, z + sign, c),
        )
    integrals[...] = jnp.zeros_like(integrals)

    own_occ = occ[i_index[own_block // 8]] + occ[j_index[z // 2]]
    row_start = pl.multiple_of((own_block % 8) * LEFT + c * LEFT_CORE, LEFT_CORE)
    row = vir[:, pl.ds(row_start, LEFT_CORE)].astype(F32) - own_occ.astype(F32)
    vir_column[...] = jnp.transpose(jnp.broadcast_to(row, (128, LEFT_CORE)))

    def invert(tile, carry):
        start = pl.multiple_of(tile * 128, 128)
        vir_row = vir[:, pl.ds(pl.multiple_of((z % 2) * RIGHT + start, 128), 128)].astype(F32)
        inverse[:, pl.ds(start, 128)] = 1.0 / ((vir_column[...] + vir_row) * (1.0 / 1024.0))
        return carry

    lax.fori_loop(0, RIGHT // 128, invert, 0)

    for half in range(2):
        for sign in (1, -1):
            wait(rights[half].at[c, place(half, 0, (-sign) % RING), pl.ds(0, 3 * ROWS)],
                 right_recv.at[half, place(half, 0, (-sign) % RING), 0])
        relay_first(half, 1)
        send_second(half, 0)
    for sign in (1, -1):
        for half in range(2):
            wait(rights[half].at[c, place(half, 0, (-sign) % RING), last],
                 right_recv.at[half, place(half, 0, (-sign) % RING), 1])
            if sign == -1:
                relay_first(half, sign)
            send_second(half, (-sign) % RING)
            share(half, place(half, 0, (-sign) % RING))
    for sign in (1, -1):
        for half in range(2):
            arrived(half, (-sign) % RING, 0)
            relay_second(half, 0, sign)
            share(half, place(half, (-sign) % RING, 0))
    for sign in (1, -1):
        wait(left.at[:, rows_of(-sign)], spread_recv.at[(-sign) % RING])
        part = 0 if sign == 1 else 1
        spots = pl.ds(part * (PLANE // 2), PLANE // 2)
        remote(
            left.at[spots, rows_of(-sign)], left.at[spots, rows_of(2)],
            spread_send, spread_recv.at[2 * part], device_of(y, x, z + sign, c),
        )
    for half in range(2):
        arrived(half, 0, 2)
        send_second(half, 2)
        share(half, place(half, 0, 2))

    for part in range(2):
        wait(left.at[pl.ds(part * (PLANE // 2), PLANE // 2), rows_of(2)], spread_recv.at[2 * part])
    remote(
        left.at[:, :, pl.ds(pl.multiple_of(other * LEFT_CORE, LEFT_CORE), LEFT_CORE)], left_all.at[c],
        core_left.at[0], core_left.at[1], sibling,
    )
    mine = pltpu.make_async_copy(
        left.at[:, :, pl.ds(pl.multiple_of(c * LEFT_CORE, LEFT_CORE), LEFT_CORE)], left_all.at[c], core_left.at[2]
    )
    mine.start()
    for first in (3, 1):
        for sign in (1, -1):
            for half in range(2):
                arrived(half, (-sign) % RING, first)
                relay_second(half, first, sign)
                share(half, place(half, (-sign) % RING, first))
                if first == 3 and sign == 1 and half == 1:
                    mine.wait()
                    wait(left_all.at[other], core_left.at[1])
                if first == 1 or sign == -1:
                    multiply(2)
    for half in range(2):
        arrived(half, 2, 0)
        share(half, place(half, 2, 0))
        multiply(2)
    for sign in (1, -1):
        for half in range(2):
            arrived(half, (-sign) % RING, 2)
            relay_second(half, 2, sign)
            share(half, place(half, (-sign) % RING, 2))
            multiply(2)
    for first in (3, 1):
        for half in range(2):
            arrived(half, 2, first)
            share(half, place(half, 2, first))
            multiply(2)
    multiply(len(ready), 0)
    final = place(0, 2, 2)
    for half in range(2):
        for part in range(2):
            block = rights[half].at[c, final, pl.ds(part * HALF_PIECE, HALF_PIECE)]
            wait(block, right_recv.at[half, final, part])
            remote(block, block, core_send.at[half], core_recv.at[half, final], sibling)
    for half in range(2):
        multiply_one(half, final, c)
    for half in range(2):
        columns = pl.ds(half * COLS, COLS)
        wait(rights[half].at[other, final], core_recv.at[half, final])
        total = integrals[:, columns] + lax.dot_general(
            left_all[other, final], rights[half][other, final], (((0,), (0,)), ((), ())), preferred_element_type=F32
        )
        amplitude[:, columns] = (total * inverse[:, columns]).astype(BF16)

    def order(step):
        spot = step * 0
        for index, entry in enumerate(ORDER):
            spot = jnp.where(step == index, entry, spot)
        return spot

    def partial_rows(owner, dz):
        start = owner * PIECE + RANK[dz] * ROWS
        return slice(start, start + ROWS)

    def multiply_back(spot):
        total = None
        for half in range(2):
            term = lax.dot_general(
                rights[half][:, spot].reshape(2 * PIECE, COLS),
                amplitude[:, half * COLS : (half + 1) * COLS],
                (((1,), (1,)), ((), ())),
                preferred_element_type=F32,
            )
            total = term if total is None else total + term
        partial[spot] = total
        for way, dz in ((0, 1), (1, -1)):
            to = device_of(y, x, z + dz, c)
            opposite[spot, way] = total[partial_rows(way, 2)].astype(BF16)
            remote(opposite.at[spot, way], relay.at[spot, way], opposite_send, relay_recv.at[spot], to)
            straight = 1 - way
            ring_out[spot, way, straight] = total[partial_rows(straight, dz % RING)].astype(BF16)
            remote(
                ring_out.at[spot, way, straight], ring_in.at[spot, way, straight], ring_send, ring_recv.at[spot], to
            )

    def pass_on(spot):
        wait(relay.at[spot], relay_recv.at[spot])
        for way, dz in ((0, 1), (1, -1)):
            total = partial[spot, partial_rows(way, dz % RING), :] + relay[spot, way].astype(F32)
            ring_out[spot, way, way] = total.astype(BF16)
            remote(
                ring_out.at[spot, way, way], ring_in.at[spot, way, way], ring_send, ring_recv.at[spot],
                device_of(y, x, z + dz, c),
            )

    own_columns = pl.ds(pl.multiple_of((own_block % 8) * LEFT + c * LEFT_CORE, LEFT_CORE), LEFT_CORE)
    own_target = gamma.at[own_block // 8, :, own_columns]

    def hand_over(spot):
        wait(ring_in.at[spot], ring_recv.at[spot])
        for owner in range(2):
            total_out[2 * spot + owner] = (
                partial[spot, partial_rows(owner, 0), :]
                + ring_in[spot, 0, owner].astype(F32)
                + ring_in[spot, 1, owner].astype(F32)
            )

    def back(step, carry):
        @pl.when(step < PLANE)
        def _():
            multiply_back(order(step))

        @pl.when((step >= RELAY_LAG) & (step < PLANE + RELAY_LAG))
        def _():
            pass_on(order(step - RELAY_LAG))

        @pl.when(step >= RELAY_LAG + RING_LAG)
        def _():
            spot = order(step - RELAY_LAG - RING_LAG)
            hand_over(spot)

            @pl.when(step < PLANE + RELAY_LAG + RING_LAG - 1)
            def _():
                for owner in range(2):
                    remote(
                        total_out.at[2 * spot + owner], own_target, total_send, gamma_recv,
                        device_of(y + spot // RING, x + spot % RING, z, owner),
                    )

        return carry

    lax.fori_loop(0, PLANE + RELAY_LAG + RING_LAG, back, 0)
    remote(total_out.at[other], own_target, total_send, gamma_recv, sibling)
    keep = pltpu.make_async_copy(total_out.at[c], own_target, held_sem)
    keep.start()
    keep.wait()
    for sem in (gamma_recv, total_send):
        wait(total_out.at[pl.ds(0, 2 * PLANE - 1)], sem)

    wait(left.at[pl.ds(0, PLANE - 1), rows_of(0)], left_send)
    wait(left.at[:, pl.ds(0, PIECE - ROWS)], spread_send)
    wait(left_all.at[c], core_left.at[0])
    for half in range(2):
        wait(rights[half].at[c, 0, pl.ds(0, PIECE - ROWS)], right_send.at[half])
        wait(rights[half].at[c, pl.ds(0, PLANE - 1)], right_send.at[half])
        wait(rights[half].at[c], core_send.at[half])
    wait(opposite, opposite_send)
    wait(ring_out, ring_send)


def copy_kernel(source, target, held, sem):
    parts = [(n, pl.ds(row, 16), row // 16) for n in range(2) for row in range(0, ROWS, 16)]
    reads = [pltpu.make_async_copy(source.at[n, rows], held.at[n, rows], sem.at[0, n, k]) for n, rows, k in parts]
    writes = [pltpu.make_async_copy(held.at[n, rows], target.at[n, rows], sem.at[1, n, k]) for n, rows, k in parts]
    for read in reads:
        read.start()
    for read, write in zip(reads, writes):
        read.wait()
        write.start()
    for write in writes:
        write.wait()


def per_device(slabs, occ_energy, vir_energy, i_index, j_index):
    anywhere = pl.BlockSpec(memory_space=pl.ANY)
    dma = pltpu.SemaphoreType.DMA
    gamma = pl.pallas_call(
        kernel,
        out_shape=jax.ShapeDtypeStruct((2, ROWS, NVIR), F32),
        in_specs=[anywhere] * 5,
        out_specs=anywhere,
        scratch_shapes=[
            pltpu.VMEM((8, ROWS, NVIR), BF16),
            pltpu.VMEM((1, NVIR), jnp.int32),
            pltpu.SMEM((8,), jnp.int32),
            pltpu.SMEM((2,), jnp.int32),
            pltpu.SMEM((2,), jnp.int32),
            pltpu.VMEM((2, ROWS, NVIR), BF16),
            pltpu.VMEM((2, ROWS, NVIR), BF16),
            pltpu.VMEM((PLANE, PIECE, LEFT), BF16),
            pltpu.VMEM((2, PLANE, PIECE, LEFT_CORE), BF16),
            pltpu.VMEM((2, PLANE, PIECE, COLS), BF16),
            pltpu.VMEM((2, PLANE, PIECE, COLS), BF16),
            pltpu.VMEM((LEFT_CORE, RIGHT), F32),
            pltpu.VMEM((LEFT_CORE, RIGHT), BF16),
            pltpu.VMEM((LEFT_CORE, 128), F32),
            pltpu.VMEM((LEFT_CORE, RIGHT), F32),
            pltpu.VMEM((PLANE, 2 * PIECE, LEFT_CORE), F32),
            pltpu.VMEM((PLANE, 2, ROWS, LEFT_CORE), BF16),
            pltpu.VMEM((PLANE, 2, ROWS, LEFT_CORE), BF16),
            pltpu.VMEM((PLANE, 2, 2, ROWS, LEFT_CORE), BF16),
            pltpu.VMEM((PLANE, 2, 2, ROWS, LEFT_CORE), BF16),
            pltpu.VMEM((2 * PLANE, ROWS, LEFT_CORE), F32),
            dma, dma((5,)), dma, dma, dma, dma((RING,)), dma((3,)), dma((2,)), dma((2, 2)), dma((2, PLANE, 2)),
            dma((2,)), dma((2, PLANE)), dma, dma((PLANE,)), dma, dma((PLANE,)), dma, dma,
        ],
        compiler_params=pltpu.CompilerParams(
            collective_id=0, has_side_effects=True, vmem_limit_bytes=60 * 2**20
        ),
        name="back_transform",
    )(slabs, vir_energy.reshape(1, NVIR), occ_energy, i_index, j_index)
    return pl.pallas_call(
        copy_kernel,
        out_shape=jax.ShapeDtypeStruct((2, ROWS, NVIR), F32),
        in_specs=[anywhere],
        out_specs=anywhere,
        scratch_shapes=[pltpu.VMEM((2, ROWS, NVIR), F32), dma((2, 2, ROWS // 16))],
        name="result",
    )(gamma)


def solution(mesh):
    placed = (P(None, ("aux", "pan"), None), P(), P(), P(), P())
    return jax.shard_map(
        per_device,
        mesh=mesh,
        in_specs=placed,
        out_specs=P(None, ("aux", "pan"), None),
        check_vma=False,
    )
```

```python
import jax
import jax.numpy as jnp
from jax import lax
from jax.experimental import pallas as pl
from jax.experimental.pallas import tpu as pltpu
from jax.sharding import PartitionSpec as P

MESH = pl.DeviceIdType.MESH
RING = 4
PLANE = RING * RING
ROWS = 48
NVIR = 4096
PIECE = RING * ROWS
HALF_PIECE = PIECE // 2
LEFT = 512
LEFT_CORE = LEFT // 2
RIGHT = 2048
COLS = RIGHT // 2
F32 = jnp.float32
BF16 = jnp.bfloat16
RELAY_LAG = 4
RING_LAG = 4
RANK = (0, 1, 3, 2)
ORDER = (10, 9, 11, 6, 14, 5, 15, 7, 13, 2, 8, 1, 3, 4, 12, 0)


def device_of(y, x, z, c):
    return ((y % RING) * 8 + (x % RING) * 2 + (z % RING) // 2, (z % 2) * 2 + c)


def rows_of(dz):
    return pl.ds(RANK[dz % RING] * ROWS, ROWS)


def kernel(
    slabs, vir_in, occ_in, i_in, j_in, gamma,
    held, vir, occ, i_index, j_index, left_own, right_own, left, left_all, right_a, right_b, integrals, amplitude, vir_column, inverse,
    partial, opposite, relay, ring_out, ring_in, total_out,
    held_sem, fetch_sem, left_send, left_recv, spread_send, spread_recv, core_left, right_send, right_first, right_recv,
    core_send, core_recv, opposite_send, relay_recv, ring_send, ring_recv, total_send, gamma_recv,
):
    aux, pan = lax.axis_index("aux"), lax.axis_index("pan")
    y, x = aux // 8, (aux // 2) % RING
    z, c = (aux % 2) * 2 + pan // 2, pan % 2
    other = 1 - c
    sibling = device_of(y, x, z, other)
    rights = (right_a, right_b)
    own_block = y * RING + x

    def remote(src, dst, send, recv, to):
        copy = pltpu.make_async_remote_copy(
            src_ref=src, dst_ref=dst, send_sem=send, recv_sem=recv, device_id=to, device_id_type=MESH
        )
        copy.start()

    def wait(ref, sem):
        pltpu.make_async_copy(ref, ref, sem).wait()

    fetches = [
        pltpu.make_async_copy(source, target, fetch_sem.at[index])
        for index, (source, target) in enumerate(
            ((j_in, j_index), (i_in, i_index), (occ_in, occ), (vir_in, vir), (slabs, held))
        )
    ]
    for fetch in fetches:
        fetch.start()
    barrier = pltpu.get_barrier_semaphore()

    def greet(to):
        pl.semaphore_signal(barrier, inc=1, device_id=to, device_id_type=MESH)

    for dz in range(1, RING):
        greet(device_of(y, x, z + dz, c))
    greet(sibling)
    for spot in range(1, PLANE):
        greet(device_of(y + spot // RING, x + spot % RING, z, c))
    for fetch in fetches:
        fetch.wait()
    for slot in range(2):
        right_own[slot] = held[j_index[slot]]
    for slot in range(2):
        left_own[slot] = held[i_index[slot]]
    pl.semaphore_wait(barrier, RING - 1 + 1 + (PLANE - 1))

    def right_columns(to, half):
        return right_own.at[to // 2, :, pl.ds(pl.multiple_of((to % 2) * RIGHT + half * COLS, COLS), COLS)]

    def exchange(dz, half):
        remote(
            right_columns((z + dz) % RING, half), rights[half].at[c, 0, rows_of(-dz)], right_send.at[half],
            right_first.at[half, 1 if dz == 2 else 0], device_of(y, x, z + dz, c),
        )

    def place(half, second, first):
        return second * RING + first if half == 0 else first * RING + second

    def toward(half, second, first):
        return device_of(y + second, x + first, z, c) if half == 0 else device_of(y + first, x + second, z, c)

    def send_first(half, rows, part):
        for sign in (1, -1):
            spot = place(half, 0, (-sign) % RING)
            remote(
                rights[half].at[c, 0, rows], rights[half].at[c, spot, rows], right_send.at[half],
                right_recv.at[half, spot, part], toward(half, 0, sign),
            )

    def relay_first(half, sign):
        here, there = place(half, 0, (-sign) % RING), place(half, 0, 2)
        part = 0 if sign == 1 else 1
        rows = pl.ds(part * HALF_PIECE, HALF_PIECE)
        remote(
            rights[half].at[c, here, rows], rights[half].at[c, there, rows], right_send.at[half],
            right_recv.at[half, there, part], toward(half, 0, sign),
        )

    def send_second(half, first, rows=pl.ds(0, PIECE)):
        here = place(half, 0, first)
        for sign in (1, -1):
            there = place(half, (-sign) % RING, first)
            remote(
                rights[half].at[c, here, rows], rights[half].at[c, there, rows], right_send.at[half],
                right_recv.at[half, there, 0], toward(half, sign, 0),
            )

    def relay_second(half, first, sign):
        here, there = place(half, (-sign) % RING, first), place(half, 2, first)
        part = 0 if sign == 1 else 1
        rows = pl.ds(part * HALF_PIECE, HALF_PIECE)
        remote(
            rights[half].at[c, here, rows], rights[half].at[c, there, rows], right_send.at[half],
            right_recv.at[half, there, part], toward(half, sign, 0),
        )

    def arrived(half, second, first):
        spot = place(half, second, first)
        if second == 2 or (second == 0 and first == 2):
            for part in range(2):
                wait(rights[half].at[c, spot, pl.ds(part * HALF_PIECE, HALF_PIECE)], right_recv.at[half, spot, part])
        else:
            wait(rights[half].at[c, spot], right_recv.at[half, spot, 0])

    ready = []

    def share(half, spot):
        block = rights[half].at[c, spot]
        remote(block, block, core_send.at[half], core_recv.at[half, spot], sibling)
        ready.append((half, spot))

    def multiply_one(half, spot, owner):
        columns = pl.ds(half * COLS, COLS)
        integrals[:, columns] += lax.dot_general(
            left_all[owner, spot], rights[half][owner, spot], (((0,), (0,)), ((), ())), preferred_element_type=F32
        )

    def multiply(limit, keep=2):
        for _ in range(limit):
            if len(ready) <= keep:
                return
            half, spot = ready.pop(0)

            def body(turn, carry):
                owner = (c + turn) % 2

                @pl.when(turn == 1)
                def _():
                    wait(rights[half].at[other, spot], core_recv.at[half, spot])

                multiply_one(half, spot, owner)
                return carry

            lax.fori_loop(0, 2, body, 0)

    for dz in (1, 3, 2):
        for half in range(2):
            exchange(dz, half)
    for step in range(1, PLANE):
        spot = (step * 5) % PLANE
        dy, dx = spot // RING, spot % RING
        block = ((y + dy) % RING) * RING + (x + dx) % RING
        remote(
            left_own.at[block // 8, :, pl.ds(pl.multiple_of((block % 8) * LEFT, LEFT), LEFT)],
            left.at[((-dy) % RING) * RING + (-dx) % RING, rows_of(0)],
            left_send,
            left_recv,
            device_of(y + dy, x + dx, z, c),
        )
    left[0, 0:ROWS, :] = left_own[own_block // 8, :, pl.ds(pl.multiple_of((own_block % 8) * LEFT, LEFT), LEFT)]

    for half in range(2):
        rights[half][c, 0, 0:ROWS, :] = right_own[
            z // 2, :, pl.ds(pl.multiple_of((z % 2) * RIGHT + half * COLS, COLS), COLS)
        ]
        send_first(half, pl.ds(0, ROWS), 0)

    middle, last = pl.ds(ROWS, 2 * ROWS), pl.ds(3 * ROWS, ROWS)
    for half in range(2):
        wait(rights[half].at[c, 0, middle], right_first.at[half, 0])
        send_first(half, middle, 0)
    for half in range(2):
        wait(rights[half].at[c, 0, last], right_first.at[half, 1])
        send_first(half, last, 1)
        share(half, 0)
    wait(left.at[pl.ds(0, PLANE - 1), rows_of(0)], left_recv)
    for sign in (1, -1):
        remote(
            left.at[:, rows_of(0)], left.at[:, rows_of(-sign)],
            spread_send, spread_recv.at[(-sign) % RING], device_of(y, x, z + sign, c),
        )
    integrals[...] = jnp.zeros_like(integrals)

    own_occ = occ[i_index[own_block // 8]] + occ[j_index[z // 2]]
    row_start = pl.multiple_of((own_block % 8) * LEFT + c * LEFT_CORE, LEFT_CORE)
    row = vir[:, pl.ds(row_start, LEFT_CORE)].astype(F32) - own_occ.astype(F32)
    vir_column[...] = jnp.transpose(jnp.broadcast_to(row, (128, LEFT_CORE)))

    def invert(tile, carry):
        start = pl.multiple_of(tile * 128, 128)
        vir_row = vir[:, pl.ds(pl.multiple_of((z % 2) * RIGHT + start, 128), 128)].astype(F32)
        inverse[:, pl.ds(start, 128)] = 1.0 / ((vir_column[...] + vir_row) * (1.0 / 1024.0))
        return carry

    lax.fori_loop(0, RIGHT // 128, invert, 0)

    for half in range(2):
        for sign in (1, -1):
            wait(rights[half].at[c, place(half, 0, (-sign) % RING), pl.ds(0, 3 * ROWS)],
                 right_recv.at[half, place(half, 0, (-sign) % RING), 0])
        relay_first(half, 1)
        send_second(half, 0)
    for sign in (1, -1):
        for half in range(2):
            wait(rights[half].at[c, place(half, 0, (-sign) % RING), last],
                 right_recv.at[half, place(half, 0, (-sign) % RING), 1])
            if sign == -1:
                relay_first(half, sign)
            send_second(half, (-sign) % RING)
            share(half, place(half, 0, (-sign) % RING))
    for sign in (1, -1):
        for half in range(2):
            arrived(half, (-sign) % RING, 0)
            relay_second(half, 0, sign)
            share(half, place(half, (-sign) % RING, 0))
    for sign in (1, -1):
        wait(left.at[:, rows_of(-sign)], spread_recv.at[(-sign) % RING])
        part = 0 if sign == 1 else 1
        spots = pl.ds(part * (PLANE // 2), PLANE // 2)
        remote(
            left.at[spots, rows_of(-sign)], left.at[spots, rows_of(2)],
            spread_send, spread_recv.at[2 * part], device_of(y, x, z + sign, c),
        )
    for half in range(2):
        arrived(half, 0, 2)
        send_second(half, 2)
        share(half, place(half, 0, 2))

    for part in range(2):
        wait(left.at[pl.ds(part * (PLANE // 2), PLANE // 2), rows_of(2)], spread_recv.at[2 * part])
    remote(
        left.at[:, :, pl.ds(pl.multiple_of(other * LEFT_CORE, LEFT_CORE), LEFT_CORE)], left_all.at[c],
        core_left.at[0], core_left.at[1], sibling,
    )
    mine = pltpu.make_async_copy(
        left.at[:, :, pl.ds(pl.multiple_of(c * LEFT_CORE, LEFT_CORE), LEFT_CORE)], left_all.at[c], core_left.at[2]
    )
    mine.start()
    for first in (3, 1):
        for sign in (1, -1):
            for half in range(2):
                arrived(half, (-sign) % RING, first)
                relay_second(half, first, sign)
                share(half, place(half, (-sign) % RING, first))
                if first == 3 and sign == 1 and half == 1:
                    mine.wait()
                    wait(left_all.at[other], core_left.at[1])
                if first == 1 or sign == -1:
                    multiply(2)
    for half in range(2):
        arrived(half, 2, 0)
        share(half, place(half, 2, 0))
        multiply(2)
    for sign in (1, -1):
        for half in range(2):
            arrived(half, (-sign) % RING, 2)
            relay_second(half, 2, sign)
            share(half, place(half, (-sign) % RING, 2))
            multiply(2)
    for first in (3, 1):
        for half in range(2):
            arrived(half, 2, first)
            share(half, place(half, 2, first))
            multiply(2)
    multiply(len(ready), 0)
    final = place(0, 2, 2)
    for half in range(2):
        for part in range(2):
            block = rights[half].at[c, final, pl.ds(part * HALF_PIECE, HALF_PIECE)]
            wait(block, right_recv.at[half, final, part])
            remote(block, block, core_send.at[half], core_recv.at[half, final], sibling)
    for half in range(2):
        multiply_one(half, final, c)
    for half in range(2):
        columns = pl.ds(half * COLS, COLS)
        wait(rights[half].at[other, final], core_recv.at[half, final])
        total = integrals[:, columns] + lax.dot_general(
            left_all[other, final], rights[half][other, final], (((0,), (0,)), ((), ())), preferred_element_type=F32
        )
        amplitude[:, columns] = (total * inverse[:, columns]).astype(BF16)

    def order(step):
        spot = step * 0
        for index, entry in enumerate(ORDER):
            spot = jnp.where(step == index, entry, spot)
        return spot

    def partial_rows(owner, dz):
        start = owner * PIECE + RANK[dz] * ROWS
        return slice(start, start + ROWS)

    def multiply_back(spot):
        total = None
        for half in range(2):
            term = lax.dot_general(
                rights[half][:, spot].reshape(2 * PIECE, COLS),
                amplitude[:, half * COLS : (half + 1) * COLS],
                (((1,), (1,)), ((), ())),
                preferred_element_type=F32,
            )
            total = term if total is None else total + term
        partial[spot] = total
        for way, dz in ((0, 1), (1, -1)):
            straight = 1 - way
            opposite[spot, way, 0] = total[partial_rows(way, 2)].astype(BF16)
            opposite[spot, way, 1] = total[partial_rows(straight, dz % RING)].astype(BF16)
            remote(
                opposite.at[spot, way], relay.at[spot, way], opposite_send, relay_recv.at[spot],
                device_of(y, x, z + dz, c),
            )

    def pass_on(spot):
        wait(relay.at[spot], relay_recv.at[spot])
        for way, dz in ((0, 1), (1, -1)):
            total = partial[spot, partial_rows(way, dz % RING), :] + relay[spot, way, 0].astype(F32)
            ring_out[spot, way] = total.astype(BF16)
            remote(
                ring_out.at[spot, way], ring_in.at[spot, way], ring_send, ring_recv.at[spot],
                device_of(y, x, z + dz, c),
            )

    own_columns = pl.ds(pl.multiple_of((own_block % 8) * LEFT + c * LEFT_CORE, LEFT_CORE), LEFT_CORE)
    own_target = gamma.at[own_block // 8, :, own_columns]

    def hand_over(spot):
        wait(ring_in.at[spot], ring_recv.at[spot])
        for owner in range(2):
            total_out[2 * spot + owner] = (
                partial[spot, partial_rows(owner, 0), :]
                + ring_in[spot, owner].astype(F32)
                + relay[spot, 1 - owner, 1].astype(F32)
            )

    def back(step, carry):
        @pl.when(step < PLANE)
        def _():
            multiply_back(order(step))

        @pl.when((step >= RELAY_LAG) & (step < PLANE + RELAY_LAG))
        def _():
            pass_on(order(step - RELAY_LAG))

        @pl.when(step >= RELAY_LAG + RING_LAG)
        def _():
            spot = order(step - RELAY_LAG - RING_LAG)
            hand_over(spot)

            @pl.when(step < PLANE + RELAY_LAG + RING_LAG - 1)
            def _():
                for owner in range(2):
                    remote(
                        total_out.at[2 * spot + owner], own_target, total_send, gamma_recv,
                        device_of(y + spot // RING, x + spot % RING, z, owner),
                    )

        return carry

    lax.fori_loop(0, PLANE + RELAY_LAG + RING_LAG, back, 0)
    remote(total_out.at[other], own_target, total_send, gamma_recv, sibling)
    keep = pltpu.make_async_copy(total_out.at[c], own_target, held_sem)
    keep.start()
    keep.wait()
    for sem in (gamma_recv, total_send):
        wait(total_out.at[pl.ds(0, 2 * PLANE - 1)], sem)

    wait(left.at[pl.ds(0, PLANE - 1), rows_of(0)], left_send)
    wait(left.at[:, pl.ds(0, PIECE - ROWS)], spread_send)
    wait(left_all.at[c], core_left.at[0])
    for half in range(2):
        wait(rights[half].at[c, 0, pl.ds(0, PIECE - ROWS)], right_send.at[half])
        wait(rights[half].at[c, pl.ds(0, PLANE - 1)], right_send.at[half])
        wait(rights[half].at[c], core_send.at[half])
    wait(opposite, opposite_send)
    wait(ring_out, ring_send)


def copy_kernel(source, target, held, sem):
    parts = [(n, pl.ds(row, 16), row // 16) for n in range(2) for row in range(0, ROWS, 16)]
    reads = [pltpu.make_async_copy(source.at[n, rows], held.at[n, rows], sem.at[0, n, k]) for n, rows, k in parts]
    writes = [pltpu.make_async_copy(held.at[n, rows], target.at[n, rows], sem.at[1, n, k]) for n, rows, k in parts]
    for read in reads:
        read.start()
    for read, write in zip(reads, writes):
        read.wait()
        write.start()
    for write in writes:
        write.wait()


def per_device(slabs, occ_energy, vir_energy, i_index, j_index):
    anywhere = pl.BlockSpec(memory_space=pl.ANY)
    dma = pltpu.SemaphoreType.DMA
    gamma = pl.pallas_call(
        kernel,
        out_shape=jax.ShapeDtypeStruct((2, ROWS, NVIR), F32),
        in_specs=[anywhere] * 5,
        out_specs=anywhere,
        scratch_shapes=[
            pltpu.VMEM((8, ROWS, NVIR), BF16),
            pltpu.VMEM((1, NVIR), jnp.int32),
            pltpu.SMEM((8,), jnp.int32),
            pltpu.SMEM((2,), jnp.int32),
            pltpu.SMEM((2,), jnp.int32),
            pltpu.VMEM((2, ROWS, NVIR), BF16),
            pltpu.VMEM((2, ROWS, NVIR), BF16),
            pltpu.VMEM((PLANE, PIECE, LEFT), BF16),
            pltpu.VMEM((2, PLANE, PIECE, LEFT_CORE), BF16),
            pltpu.VMEM((2, PLANE, PIECE, COLS), BF16),
            pltpu.VMEM((2, PLANE, PIECE, COLS), BF16),
            pltpu.VMEM((LEFT_CORE, RIGHT), F32),
            pltpu.VMEM((LEFT_CORE, RIGHT), BF16),
            pltpu.VMEM((LEFT_CORE, 128), F32),
            pltpu.VMEM((LEFT_CORE, RIGHT), F32),
            pltpu.VMEM((PLANE, 2 * PIECE, LEFT_CORE), F32),
            pltpu.VMEM((PLANE, 2, 2, ROWS, LEFT_CORE), BF16),
            pltpu.VMEM((PLANE, 2, 2, ROWS, LEFT_CORE), BF16),
            pltpu.VMEM((PLANE, 2, ROWS, LEFT_CORE), BF16),
            pltpu.VMEM((PLANE, 2, ROWS, LEFT_CORE), BF16),
            pltpu.VMEM((2 * PLANE, ROWS, LEFT_CORE), F32),
            dma, dma((5,)), dma, dma, dma, dma((RING,)), dma((3,)), dma((2,)), dma((2, 2)), dma((2, PLANE, 2)),
            dma((2,)), dma((2, PLANE)), dma, dma((PLANE,)), dma, dma((PLANE,)), dma, dma,
        ],
        compiler_params=pltpu.CompilerParams(
            collective_id=0, has_side_effects=True, vmem_limit_bytes=60 * 2**20
        ),
        name="back_transform",
    )(slabs, vir_energy.reshape(1, NVIR), occ_energy, i_index, j_index)
    return pl.pallas_call(
        copy_kernel,
        out_shape=jax.ShapeDtypeStruct((2, ROWS, NVIR), F32),
        in_specs=[anywhere],
        out_specs=anywhere,
        scratch_shapes=[pltpu.VMEM((2, ROWS, NVIR), F32), dma((2, 2, ROWS // 16))],
        name="result",
    )(gamma)


def solution(mesh):
    placed = (P(None, ("aux", "pan"), None), P(), P(), P(), P())
    return jax.shard_map(
        per_device,
        mesh=mesh,
        in_specs=placed,
        out_specs=P(None, ("aux", "pan"), None),
        check_vma=False,
    )
```

```python
import jax
import jax.numpy as jnp
from jax import lax
from jax.experimental import pallas as pl
from jax.experimental.pallas import tpu as pltpu
from jax.sharding import PartitionSpec as P

MESH = pl.DeviceIdType.MESH
RING = 4
PLANE = RING * RING
ROWS = 48
NVIR = 4096
PIECE = RING * ROWS
HALF_PIECE = PIECE // 2
LEFT = 512
LEFT_CORE = LEFT // 2
RIGHT = 2048
COLS = RIGHT // 2
F32 = jnp.float32
BF16 = jnp.bfloat16
RELAY_LAG = 4
RING_LAG = 4
RANK = (0, 1, 3, 2)
ORDER = (10, 9, 11, 6, 14, 5, 15, 7, 13, 2, 8, 1, 3, 4, 12, 0)


def device_of(y, x, z, c):
    return ((y % RING) * 8 + (x % RING) * 2 + (z % RING) // 2, (z % 2) * 2 + c)


def rows_of(dz):
    return pl.ds(RANK[dz % RING] * ROWS, ROWS)


def kernel(
    slabs, vir_in, occ_in, i_in, j_in, gamma,
    held, vir, occ, i_index, j_index, left_own, right_own, left, left_all, right_a, right_b, integrals, amplitude, vir_column, inverse,
    partial, opposite, relay, ring_out, ring_in, total_out,
    held_sem, fetch_sem, left_send, left_recv, spread_send, spread_recv, core_left, right_send, right_first, right_recv,
    core_send, core_recv, opposite_send, relay_recv, ring_send, ring_recv, total_send, gamma_recv,
):
    aux, pan = lax.axis_index("aux"), lax.axis_index("pan")
    y, x = aux // 8, (aux // 2) % RING
    z, c = (aux % 2) * 2 + pan // 2, pan % 2
    other = 1 - c
    sibling = device_of(y, x, z, other)
    rights = (right_a, right_b)
    own_block = y * RING + x

    def remote(src, dst, send, recv, to):
        copy = pltpu.make_async_remote_copy(
            src_ref=src, dst_ref=dst, send_sem=send, recv_sem=recv, device_id=to, device_id_type=MESH
        )
        copy.start()

    def wait(ref, sem):
        pltpu.make_async_copy(ref, ref, sem).wait()

    fetches = [
        pltpu.make_async_copy(source, target, fetch_sem.at[index])
        for index, (source, target) in enumerate(
            ((j_in, j_index), (i_in, i_index), (occ_in, occ), (vir_in, vir), (slabs, held))
        )
    ]
    for fetch in fetches:
        fetch.start()
    barrier = pltpu.get_barrier_semaphore()

    def greet(to):
        pl.semaphore_signal(barrier, inc=1, device_id=to, device_id_type=MESH)

    for dz in range(1, RING):
        greet(device_of(y, x, z + dz, c))
    greet(sibling)
    for spot in range(1, PLANE):
        greet(device_of(y + spot // RING, x + spot % RING, z, c))
    for fetch in fetches:
        fetch.wait()
    for slot in range(2):
        right_own[slot] = held[j_index[slot]]
    for slot in range(2):
        left_own[slot] = held[i_index[slot]]
    pl.semaphore_wait(barrier, RING - 1 + 1 + (PLANE - 1))

    def right_columns(to, half):
        return right_own.at[to // 2, :, pl.ds(pl.multiple_of((to % 2) * RIGHT + half * COLS, COLS), COLS)]

    def exchange(dz, half):
        remote(
            right_columns((z + dz) % RING, half), rights[half].at[c, 0, rows_of(-dz)], right_send.at[half],
            right_first.at[half, 1 if dz == 2 else 0], device_of(y, x, z + dz, c),
        )

    def place(half, second, first):
        return second * RING + first if half == 0 else first * RING + second

    def toward(half, second, first):
        return device_of(y + second, x + first, z, c) if half == 0 else device_of(y + first, x + second, z, c)

    def send_first(half, rows, part):
        for sign in (1, -1):
            spot = place(half, 0, (-sign) % RING)
            remote(
                rights[half].at[c, 0, rows], rights[half].at[c, spot, rows], right_send.at[half],
                right_recv.at[half, spot, part], toward(half, 0, sign),
            )

    def relay_first(half, sign):
        here, there = place(half, 0, (-sign) % RING), place(half, 0, 2)
        part = 0 if sign == 1 else 1
        rows = pl.ds(part * HALF_PIECE, HALF_PIECE)
        remote(
            rights[half].at[c, here, rows], rights[half].at[c, there, rows], right_send.at[half],
            right_recv.at[half, there, part], toward(half, 0, sign),
        )

    def send_second(half, first, rows=pl.ds(0, PIECE)):
        here = place(half, 0, first)
        for sign in (1, -1):
            there = place(half, (-sign) % RING, first)
            remote(
                rights[half].at[c, here, rows], rights[half].at[c, there, rows], right_send.at[half],
                right_recv.at[half, there, 0], toward(half, sign, 0),
            )

    def relay_second(half, first, sign):
        here, there = place(half, (-sign) % RING, first), place(half, 2, first)
        part = 0 if sign == 1 else 1
        rows = pl.ds(part * HALF_PIECE, HALF_PIECE)
        remote(
            rights[half].at[c, here, rows], rights[half].at[c, there, rows], right_send.at[half],
            right_recv.at[half, there, part], toward(half, sign, 0),
        )

    def arrived(half, second, first):
        spot = place(half, second, first)
        if second == 2 or (second == 0 and first == 2):
            for part in range(2):
                wait(rights[half].at[c, spot, pl.ds(part * HALF_PIECE, HALF_PIECE)], right_recv.at[half, spot, part])
        else:
            wait(rights[half].at[c, spot], right_recv.at[half, spot, 0])

    ready = []

    def share(half, spot):
        block = rights[half].at[c, spot]
        remote(block, block, core_send.at[half], core_recv.at[half, spot], sibling)
        ready.append((half, spot))

    def multiply_one(half, spot, owner):
        columns = pl.ds(half * COLS, COLS)
        integrals[:, columns] += lax.dot_general(
            left_all[owner, spot], rights[half][owner, spot], (((0,), (0,)), ((), ())), preferred_element_type=F32
        )

    def multiply(limit, keep=2):
        for _ in range(limit):
            if len(ready) <= keep:
                return
            half, spot = ready.pop(0)

            def body(turn, carry):
                owner = (c + turn) % 2

                @pl.when(turn == 1)
                def _():
                    wait(rights[half].at[other, spot], core_recv.at[half, spot])

                multiply_one(half, spot, owner)
                return carry

            lax.fori_loop(0, 2, body, 0)

    for dz in (1, 3, 2):
        for half in range(2):
            exchange(dz, half)
    for step in range(1, PLANE):
        spot = (step * 5) % PLANE
        dy, dx = spot // RING, spot % RING
        block = ((y + dy) % RING) * RING + (x + dx) % RING
        remote(
            left_own.at[block // 8, :, pl.ds(pl.multiple_of((block % 8) * LEFT, LEFT), LEFT)],
            left.at[((-dy) % RING) * RING + (-dx) % RING, rows_of(0)],
            left_send,
            left_recv,
            device_of(y + dy, x + dx, z, c),
        )
    left[0, 0:ROWS, :] = left_own[own_block // 8, :, pl.ds(pl.multiple_of((own_block % 8) * LEFT, LEFT), LEFT)]

    for half in range(2):
        rights[half][c, 0, 0:ROWS, :] = right_own[
            z // 2, :, pl.ds(pl.multiple_of((z % 2) * RIGHT + half * COLS, COLS), COLS)
        ]
        send_first(half, pl.ds(0, ROWS), 0)

    middle, last = pl.ds(ROWS, 2 * ROWS), pl.ds(3 * ROWS, ROWS)
    for half in range(2):
        wait(rights[half].at[c, 0, middle], right_first.at[half, 0])
        send_first(half, middle, 0)
    for half in range(2):
        wait(rights[half].at[c, 0, last], right_first.at[half, 1])
        send_first(half, last, 1)
        share(half, 0)
    wait(left.at[pl.ds(0, PLANE - 1), rows_of(0)], left_recv)
    for sign in (1, -1):
        remote(
            left.at[:, rows_of(0)], left.at[:, rows_of(-sign)],
            spread_send, spread_recv.at[(-sign) % RING], device_of(y, x, z + sign, c),
        )
    integrals[...] = jnp.zeros_like(integrals)

    own_occ = occ[i_index[own_block // 8]] + occ[j_index[z // 2]]
    row_start = pl.multiple_of((own_block % 8) * LEFT + c * LEFT_CORE, LEFT_CORE)
    row = vir[:, pl.ds(row_start, LEFT_CORE)].astype(F32) - own_occ.astype(F32)
    vir_column[...] = jnp.transpose(jnp.broadcast_to(row, (128, LEFT_CORE)))

    def invert(tile, carry):
        start = pl.multiple_of(tile * 128, 128)
        vir_row = vir[:, pl.ds(pl.multiple_of((z % 2) * RIGHT + start, 128), 128)].astype(F32)
        inverse[:, pl.ds(start, 128)] = 1.0 / ((vir_column[...] + vir_row) * (1.0 / 1024.0))
        return carry

    lax.fori_loop(0, RIGHT // 128, invert, 0)

    for half in range(2):
        for sign in (1, -1):
            wait(rights[half].at[c, place(half, 0, (-sign) % RING), pl.ds(0, 3 * ROWS)],
                 right_recv.at[half, place(half, 0, (-sign) % RING), 0])
        relay_first(half, 1)
        send_second(half, 0)
    for sign in (1, -1):
        for half in range(2):
            wait(rights[half].at[c, place(half, 0, (-sign) % RING), last],
                 right_recv.at[half, place(half, 0, (-sign) % RING), 1])
            if sign == -1:
                relay_first(half, sign)
            send_second(half, (-sign) % RING)
            share(half, place(half, 0, (-sign) % RING))
    for sign in (1, -1):
        for half in range(2):
            arrived(half, (-sign) % RING, 0)
            relay_second(half, 0, sign)
            share(half, place(half, (-sign) % RING, 0))
    for sign in (1, -1):
        wait(left.at[:, rows_of(-sign)], spread_recv.at[(-sign) % RING])
        part = 0 if sign == 1 else 1
        spots = pl.ds(part * (PLANE // 2), PLANE // 2)
        remote(
            left.at[spots, rows_of(-sign)], left.at[spots, rows_of(2)],
            spread_send, spread_recv.at[2 * part], device_of(y, x, z + sign, c),
        )
    for half in range(2):
        arrived(half, 0, 2)
        send_second(half, 2)
        share(half, place(half, 0, 2))

    for part in range(2):
        wait(left.at[pl.ds(part * (PLANE // 2), PLANE // 2), rows_of(2)], spread_recv.at[2 * part])
    remote(
        left.at[:, :, pl.ds(pl.multiple_of(other * LEFT_CORE, LEFT_CORE), LEFT_CORE)], left_all.at[c],
        core_left.at[0], core_left.at[1], sibling,
    )
    mine = pltpu.make_async_copy(
        left.at[:, :, pl.ds(pl.multiple_of(c * LEFT_CORE, LEFT_CORE), LEFT_CORE)], left_all.at[c], core_left.at[2]
    )
    mine.start()
    for first in (3, 1):
        for sign in (1, -1):
            for half in range(2):
                arrived(half, (-sign) % RING, first)
                relay_second(half, first, sign)
                share(half, place(half, (-sign) % RING, first))
                if first == 3 and sign == 1 and half == 1:
                    mine.wait()
                    wait(left_all.at[other], core_left.at[1])
                if first == 1 or sign == -1:
                    multiply(2)
    for half in range(2):
        arrived(half, 2, 0)
        share(half, place(half, 2, 0))
        multiply(2)
    for sign in (1, -1):
        for half in range(2):
            arrived(half, (-sign) % RING, 2)
            relay_second(half, 2, sign)
            share(half, place(half, (-sign) % RING, 2))
            multiply(2)
    for first in (3, 1):
        for half in range(2):
            arrived(half, 2, first)
            share(half, place(half, 2, first))
            multiply(2)
    multiply(len(ready), 0)
    final = place(0, 2, 2)
    for half in range(2):
        for part in range(2):
            block = rights[half].at[c, final, pl.ds(part * HALF_PIECE, HALF_PIECE)]
            wait(block, right_recv.at[half, final, part])
            remote(block, block, core_send.at[half], core_recv.at[half, final], sibling)
    for half in range(2):
        multiply_one(half, final, c)
    for half in range(2):
        columns = pl.ds(half * COLS, COLS)
        wait(rights[half].at[other, final], core_recv.at[half, final])
        total = integrals[:, columns] + lax.dot_general(
            left_all[other, final], rights[half][other, final], (((0,), (0,)), ((), ())), preferred_element_type=F32
        )
        amplitude[:, columns] = (total * inverse[:, columns]).astype(BF16)

    def order(step):
        spot = step * 0
        for index, entry in enumerate(ORDER):
            spot = jnp.where(step == index, entry, spot)
        return spot

    def partial_rows(owner, dz):
        start = owner * PIECE + RANK[dz] * ROWS
        return slice(start, start + ROWS)

    def send_relay(spot):
        for way, dz in ((0, 1), (1, -1)):
            remote(
                opposite.at[spot, way], relay.at[spot, way], opposite_send, relay_recv.at[spot],
                device_of(y, x, z + dz, c),
            )

    first_spot = ORDER[0]
    ahead = None
    for half in range(2):
        term = lax.dot_general(
            rights[half][:, first_spot, 3 * ROWS :, :].reshape(2 * ROWS, COLS),
            amplitude[:, half * COLS : (half + 1) * COLS],
            (((1,), (1,)), ((), ())),
            preferred_element_type=F32,
        )
        ahead = term if ahead is None else ahead + term
    for way in range(2):
        opposite[first_spot, way] = ahead[way * ROWS : (way + 1) * ROWS].astype(BF16)
    send_relay(first_spot)

    def multiply_back(step, spot):
        total = None
        for half in range(2):
            term = lax.dot_general(
                rights[half][:, spot].reshape(2 * PIECE, COLS),
                amplitude[:, half * COLS : (half + 1) * COLS],
                (((1,), (1,)), ((), ())),
                preferred_element_type=F32,
            )
            total = term if total is None else total + term
        partial[spot] = total
        for way, dz in ((0, 1), (1, -1)):
            to = device_of(y, x, z + dz, c)

            @pl.when(step > 0)
            def _():
                opposite[spot, way] = total[partial_rows(way, 2)].astype(BF16)
                remote(opposite.at[spot, way], relay.at[spot, way], opposite_send, relay_recv.at[spot], to)

            straight = 1 - way
            ring_out[spot, way, straight] = total[partial_rows(straight, dz % RING)].astype(BF16)
            remote(
                ring_out.at[spot, way, straight], ring_in.at[spot, way, straight], ring_send, ring_recv.at[spot], to
            )

    def pass_on(spot):
        wait(relay.at[spot], relay_recv.at[spot])
        for way, dz in ((0, 1), (1, -1)):
            total = partial[spot, partial_rows(way, dz % RING), :] + relay[spot, way].astype(F32)
            ring_out[spot, way, way] = total.astype(BF16)
            remote(
                ring_out.at[spot, way, way], ring_in.at[spot, way, way], ring_send, ring_recv.at[spot],
                device_of(y, x, z + dz, c),
            )

    own_columns = pl.ds(pl.multiple_of((own_block % 8) * LEFT + c * LEFT_CORE, LEFT_CORE), LEFT_CORE)
    own_target = gamma.at[own_block // 8, :, own_columns]

    def hand_over(spot):
        wait(ring_in.at[spot], ring_recv.at[spot])
        for owner in range(2):
            total_out[2 * spot + owner] = (
                partial[spot, partial_rows(owner, 0), :]
                + ring_in[spot, 0, owner].astype(F32)
                + ring_in[spot, 1, owner].astype(F32)
            )

    def back(step, carry):
        @pl.when(step < PLANE)
        def _():
            multiply_back(step, order(step))

        @pl.when((step >= RELAY_LAG) & (step < PLANE + RELAY_LAG))
        def _():
            pass_on(order(step - RELAY_LAG))

        @pl.when(step >= RELAY_LAG + RING_LAG)
        def _():
            spot = order(step - RELAY_LAG - RING_LAG)
            hand_over(spot)

            @pl.when(step < PLANE + RELAY_LAG + RING_LAG - 1)
            def _():
                for owner in range(2):
                    remote(
                        total_out.at[2 * spot + owner], own_target, total_send, gamma_recv,
                        device_of(y + spot // RING, x + spot % RING, z, owner),
                    )

        return carry

    lax.fori_loop(0, PLANE + RELAY_LAG + RING_LAG, back, 0)
    remote(total_out.at[other], own_target, total_send, gamma_recv, sibling)
    keep = pltpu.make_async_copy(total_out.at[c], own_target, held_sem)
    keep.start()
    keep.wait()
    for sem in (gamma_recv, total_send):
        wait(total_out.at[pl.ds(0, 2 * PLANE - 1)], sem)

    wait(left.at[pl.ds(0, PLANE - 1), rows_of(0)], left_send)
    wait(left.at[:, pl.ds(0, PIECE - ROWS)], spread_send)
    wait(left_all.at[c], core_left.at[0])
    for half in range(2):
        wait(rights[half].at[c, 0, pl.ds(0, PIECE - ROWS)], right_send.at[half])
        wait(rights[half].at[c, pl.ds(0, PLANE - 1)], right_send.at[half])
        wait(rights[half].at[c], core_send.at[half])
    wait(opposite, opposite_send)
    wait(ring_out, ring_send)


def copy_kernel(source, target, held, sem):
    parts = [(n, pl.ds(row, 16), row // 16) for n in range(2) for row in range(0, ROWS, 16)]
    reads = [pltpu.make_async_copy(source.at[n, rows], held.at[n, rows], sem.at[0, n, k]) for n, rows, k in parts]
    writes = [pltpu.make_async_copy(held.at[n, rows], target.at[n, rows], sem.at[1, n, k]) for n, rows, k in parts]
    for read in reads:
        read.start()
    for read, write in zip(reads, writes):
        read.wait()
        write.start()
    for write in writes:
        write.wait()


def per_device(slabs, occ_energy, vir_energy, i_index, j_index):
    anywhere = pl.BlockSpec(memory_space=pl.ANY)
    dma = pltpu.SemaphoreType.DMA
    gamma = pl.pallas_call(
        kernel,
        out_shape=jax.ShapeDtypeStruct((2, ROWS, NVIR), F32),
        in_specs=[anywhere] * 5,
        out_specs=anywhere,
        scratch_shapes=[
            pltpu.VMEM((8, ROWS, NVIR), BF16),
            pltpu.VMEM((1, NVIR), jnp.int32),
            pltpu.SMEM((8,), jnp.int32),
            pltpu.SMEM((2,), jnp.int32),
            pltpu.SMEM((2,), jnp.int32),
            pltpu.VMEM((2, ROWS, NVIR), BF16),
            pltpu.VMEM((2, ROWS, NVIR), BF16),
            pltpu.VMEM((PLANE, PIECE, LEFT), BF16),
            pltpu.VMEM((2, PLANE, PIECE, LEFT_CORE), BF16),
            pltpu.VMEM((2, PLANE, PIECE, COLS), BF16),
            pltpu.VMEM((2, PLANE, PIECE, COLS), BF16),
            pltpu.VMEM((LEFT_CORE, RIGHT), F32),
            pltpu.VMEM((LEFT_CORE, RIGHT), BF16),
            pltpu.VMEM((LEFT_CORE, 128), F32),
            pltpu.VMEM((LEFT_CORE, RIGHT), F32),
            pltpu.VMEM((PLANE, 2 * PIECE, LEFT_CORE), F32),
            pltpu.VMEM((PLANE, 2, ROWS, LEFT_CORE), BF16),
            pltpu.VMEM((PLANE, 2, ROWS, LEFT_CORE), BF16),
            pltpu.VMEM((PLANE, 2, 2, ROWS, LEFT_CORE), BF16),
            pltpu.VMEM((PLANE, 2, 2, ROWS, LEFT_CORE), BF16),
            pltpu.VMEM((2 * PLANE, ROWS, LEFT_CORE), F32),
            dma, dma((5,)), dma, dma, dma, dma((RING,)), dma((3,)), dma((2,)), dma((2, 2)), dma((2, PLANE, 2)),
            dma((2,)), dma((2, PLANE)), dma, dma((PLANE,)), dma, dma((PLANE,)), dma, dma,
        ],
        compiler_params=pltpu.CompilerParams(
            collective_id=0, has_side_effects=True, vmem_limit_bytes=60 * 2**20
        ),
        name="back_transform",
    )(slabs, vir_energy.reshape(1, NVIR), occ_energy, i_index, j_index)
    return pl.pallas_call(
        copy_kernel,
        out_shape=jax.ShapeDtypeStruct((2, ROWS, NVIR), F32),
        in_specs=[anywhere],
        out_specs=anywhere,
        scratch_shapes=[pltpu.VMEM((2, ROWS, NVIR), F32), dma((2, 2, ROWS // 16))],
        name="result",
    )(gamma)


def solution(mesh):
    placed = (P(None, ("aux", "pan"), None), P(), P(), P(), P())
    return jax.shard_map(
        per_device,
        mesh=mesh,
        in_specs=placed,
        out_specs=P(None, ("aux", "pan"), None),
        check_vma=False,
    )
```

```python
import jax
import jax.numpy as jnp
from jax import lax
from jax.experimental import pallas as pl
from jax.experimental.pallas import tpu as pltpu
from jax.sharding import PartitionSpec as P

MESH = pl.DeviceIdType.MESH
RING = 4
PLANE = RING * RING
ROWS = 48
NVIR = 4096
PIECE = RING * ROWS
HALF_PIECE = PIECE // 2
LEFT = 512
LEFT_CORE = LEFT // 2
RIGHT = 2048
COLS = RIGHT // 2
F32 = jnp.float32
BF16 = jnp.bfloat16
RELAY_LAG = 4
RING_LAG = 3
RANK = (0, 1, 3, 2)
ORDER = (10, 9, 11, 6, 14, 5, 15, 7, 13, 2, 8, 1, 3, 4, 12, 0)


def device_of(y, x, z, c):
    return ((y % RING) * 8 + (x % RING) * 2 + (z % RING) // 2, (z % 2) * 2 + c)


def rows_of(dz):
    return pl.ds(RANK[dz % RING] * ROWS, ROWS)


def kernel(
    slabs, vir_in, occ_in, i_in, j_in, gamma,
    held, vir, occ, i_index, j_index, left_own, right_own, left, left_all, right_a, right_b, integrals, amplitude, vir_column, inverse,
    partial, opposite, relay, ring_out, ring_in, total_out,
    held_sem, fetch_sem, left_send, left_recv, spread_send, spread_recv, core_left, right_send, right_first, right_recv,
    core_send, core_recv, opposite_send, relay_recv, ring_send, ring_recv, total_send, gamma_recv,
):
    aux, pan = lax.axis_index("aux"), lax.axis_index("pan")
    y, x = aux // 8, (aux // 2) % RING
    z, c = (aux % 2) * 2 + pan // 2, pan % 2
    other = 1 - c
    sibling = device_of(y, x, z, other)
    rights = (right_a, right_b)
    own_block = y * RING + x

    def remote(src, dst, send, recv, to):
        copy = pltpu.make_async_remote_copy(
            src_ref=src, dst_ref=dst, send_sem=send, recv_sem=recv, device_id=to, device_id_type=MESH
        )
        copy.start()

    def wait(ref, sem):
        pltpu.make_async_copy(ref, ref, sem).wait()

    fetches = [
        pltpu.make_async_copy(source, target, fetch_sem.at[index])
        for index, (source, target) in enumerate(
            ((j_in, j_index), (i_in, i_index), (occ_in, occ), (vir_in, vir), (slabs, held))
        )
    ]
    for fetch in fetches:
        fetch.start()
    barrier = pltpu.get_barrier_semaphore()

    def greet(to):
        pl.semaphore_signal(barrier, inc=1, device_id=to, device_id_type=MESH)

    for dz in range(1, RING):
        greet(device_of(y, x, z + dz, c))
    greet(sibling)
    for spot in range(1, PLANE):
        greet(device_of(y + spot // RING, x + spot % RING, z, c))
    for fetch in fetches:
        fetch.wait()
    for slot in range(2):
        right_own[slot] = held[j_index[slot]]
    for slot in range(2):
        left_own[slot] = held[i_index[slot]]
    pl.semaphore_wait(barrier, RING - 1 + 1 + (PLANE - 1))

    def right_columns(to, half):
        return right_own.at[to // 2, :, pl.ds(pl.multiple_of((to % 2) * RIGHT + half * COLS, COLS), COLS)]

    def exchange(dz, half):
        remote(
            right_columns((z + dz) % RING, half), rights[half].at[c, 0, rows_of(-dz)], right_send.at[half],
            right_first.at[half, 1 if dz == 2 else 0], device_of(y, x, z + dz, c),
        )

    def place(half, second, first):
        return second * RING + first if half == 0 else first * RING + second

    def toward(half, second, first):
        return device_of(y + second, x + first, z, c) if half == 0 else device_of(y + first, x + second, z, c)

    def send_first(half, rows, part):
        for sign in (1, -1):
            spot = place(half, 0, (-sign) % RING)
            remote(
                rights[half].at[c, 0, rows], rights[half].at[c, spot, rows], right_send.at[half],
                right_recv.at[half, spot, part], toward(half, 0, sign),
            )

    def relay_first(half, sign):
        here, there = place(half, 0, (-sign) % RING), place(half, 0, 2)
        part = 0 if sign == 1 else 1
        rows = pl.ds(part * HALF_PIECE, HALF_PIECE)
        remote(
            rights[half].at[c, here, rows], rights[half].at[c, there, rows], right_send.at[half],
            right_recv.at[half, there, part], toward(half, 0, sign),
        )

    def send_second(half, first, rows=pl.ds(0, PIECE)):
        here = place(half, 0, first)
        for sign in (1, -1):
            there = place(half, (-sign) % RING, first)
            remote(
                rights[half].at[c, here, rows], rights[half].at[c, there, rows], right_send.at[half],
                right_recv.at[half, there, 0], toward(half, sign, 0),
            )

    def relay_second(half, first, sign):
        here, there = place(half, (-sign) % RING, first), place(half, 2, first)
        part = 0 if sign == 1 else 1
        rows = pl.ds(part * HALF_PIECE, HALF_PIECE)
        remote(
            rights[half].at[c, here, rows], rights[half].at[c, there, rows], right_send.at[half],
            right_recv.at[half, there, part], toward(half, sign, 0),
        )

    def arrived(half, second, first):
        spot = place(half, second, first)
        if second == 2 or (second == 0 and first == 2):
            for part in range(2):
                wait(rights[half].at[c, spot, pl.ds(part * HALF_PIECE, HALF_PIECE)], right_recv.at[half, spot, part])
        else:
            wait(rights[half].at[c, spot], right_recv.at[half, spot, 0])

    ready = []

    def share(half, spot):
        block = rights[half].at[c, spot]
        remote(block, block, core_send.at[half], core_recv.at[half, spot], sibling)
        ready.append((half, spot))

    def multiply_one(half, spot, owner):
        columns = pl.ds(half * COLS, COLS)
        integrals[:, columns] += lax.dot_general(
            left_all[owner, spot], rights[half][owner, spot], (((0,), (0,)), ((), ())), preferred_element_type=F32
        )

    def multiply(limit, keep=2):
        for _ in range(limit):
            if len(ready) <= keep:
                return
            half, spot = ready.pop(0)

            def body(turn, carry):
                owner = (c + turn) % 2

                @pl.when(turn == 1)
                def _():
                    wait(rights[half].at[other, spot], core_recv.at[half, spot])

                multiply_one(half, spot, owner)
                return carry

            lax.fori_loop(0, 2, body, 0)

    for dz in (1, 3, 2):
        for half in range(2):
            exchange(dz, half)
    for step in range(1, PLANE):
        spot = (step * 5) % PLANE
        dy, dx = spot // RING, spot % RING
        block = ((y + dy) % RING) * RING + (x + dx) % RING
        remote(
            left_own.at[block // 8, :, pl.ds(pl.multiple_of((block % 8) * LEFT, LEFT), LEFT)],
            left.at[((-dy) % RING) * RING + (-dx) % RING, rows_of(0)],
            left_send,
            left_recv,
            device_of(y + dy, x + dx, z, c),
        )
    left[0, 0:ROWS, :] = left_own[own_block // 8, :, pl.ds(pl.multiple_of((own_block % 8) * LEFT, LEFT), LEFT)]

    for half in range(2):
        rights[half][c, 0, 0:ROWS, :] = right_own[
            z // 2, :, pl.ds(pl.multiple_of((z % 2) * RIGHT + half * COLS, COLS), COLS)
        ]
        send_first(half, pl.ds(0, ROWS), 0)

    middle, last = pl.ds(ROWS, 2 * ROWS), pl.ds(3 * ROWS, ROWS)
    for half in range(2):
        wait(rights[half].at[c, 0, middle], right_first.at[half, 0])
        send_first(half, middle, 0)
    for half in range(2):
        wait(rights[half].at[c, 0, last], right_first.at[half, 1])
        send_first(half, last, 1)
        share(half, 0)
    wait(left.at[pl.ds(0, PLANE - 1), rows_of(0)], left_recv)
    for sign in (1, -1):
        remote(
            left.at[:, rows_of(0)], left.at[:, rows_of(-sign)],
            spread_send, spread_recv.at[(-sign) % RING], device_of(y, x, z + sign, c),
        )
    integrals[...] = jnp.zeros_like(integrals)

    own_occ = occ[i_index[own_block // 8]] + occ[j_index[z // 2]]
    row_start = pl.multiple_of((own_block % 8) * LEFT + c * LEFT_CORE, LEFT_CORE)
    row = vir[:, pl.ds(row_start, LEFT_CORE)].astype(F32) - own_occ.astype(F32)
    vir_column[...] = jnp.transpose(jnp.broadcast_to(row, (128, LEFT_CORE)))

    def invert(tile, carry):
        start = pl.multiple_of(tile * 128, 128)
        vir_row = vir[:, pl.ds(pl.multiple_of((z % 2) * RIGHT + start, 128), 128)].astype(F32)
        inverse[:, pl.ds(start, 128)] = 1.0 / ((vir_column[...] + vir_row) * (1.0 / 1024.0))
        return carry

    lax.fori_loop(0, RIGHT // 128, invert, 0)

    for half in range(2):
        for sign in (1, -1):
            wait(rights[half].at[c, place(half, 0, (-sign) % RING), pl.ds(0, 3 * ROWS)],
                 right_recv.at[half, place(half, 0, (-sign) % RING), 0])
        relay_first(half, 1)
        send_second(half, 0)
    for sign in (1, -1):
        for half in range(2):
            wait(rights[half].at[c, place(half, 0, (-sign) % RING), last],
                 right_recv.at[half, place(half, 0, (-sign) % RING), 1])
            if sign == -1:
                relay_first(half, sign)
            send_second(half, (-sign) % RING)
            share(half, place(half, 0, (-sign) % RING))
    for sign in (1, -1):
        for half in range(2):
            arrived(half, (-sign) % RING, 0)
            relay_second(half, 0, sign)
            share(half, place(half, (-sign) % RING, 0))
    for sign in (1, -1):
        wait(left.at[:, rows_of(-sign)], spread_recv.at[(-sign) % RING])
        part = 0 if sign == 1 else 1
        spots = pl.ds(part * (PLANE // 2), PLANE // 2)
        remote(
            left.at[spots, rows_of(-sign)], left.at[spots, rows_of(2)],
            spread_send, spread_recv.at[2 * part], device_of(y, x, z + sign, c),
        )
    for half in range(2):
        arrived(half, 0, 2)
        send_second(half, 2)
        share(half, place(half, 0, 2))

    for part in range(2):
        wait(left.at[pl.ds(part * (PLANE // 2), PLANE // 2), rows_of(2)], spread_recv.at[2 * part])
    remote(
        left.at[:, :, pl.ds(pl.multiple_of(other * LEFT_CORE, LEFT_CORE), LEFT_CORE)], left_all.at[c],
        core_left.at[0], core_left.at[1], sibling,
    )
    mine = pltpu.make_async_copy(
        left.at[:, :, pl.ds(pl.multiple_of(c * LEFT_CORE, LEFT_CORE), LEFT_CORE)], left_all.at[c], core_left.at[2]
    )
    mine.start()
    for first in (3, 1):
        for sign in (1, -1):
            for half in range(2):
                arrived(half, (-sign) % RING, first)
                relay_second(half, first, sign)
                share(half, place(half, (-sign) % RING, first))
                if first == 3 and sign == 1 and half == 1:
                    mine.wait()
                    wait(left_all.at[other], core_left.at[1])
                if first == 1 or sign == -1:
                    multiply(2)
    for half in range(2):
        arrived(half, 2, 0)
        share(half, place(half, 2, 0))
        multiply(2)
    for sign in (1, -1):
        for half in range(2):
            arrived(half, (-sign) % RING, 2)
            relay_second(half, 2, sign)
            share(half, place(half, (-sign) % RING, 2))
            multiply(2)
    for first in (3, 1):
        for half in range(2):
            arrived(half, 2, first)
            share(half, place(half, 2, first))
            multiply(2)
    multiply(len(ready), 0)
    final = place(0, 2, 2)
    for half in range(2):
        for part in range(2):
            block = rights[half].at[c, final, pl.ds(part * HALF_PIECE, HALF_PIECE)]
            wait(block, right_recv.at[half, final, part])
            remote(block, block, core_send.at[half], core_recv.at[half, final], sibling)
    for half in range(2):
        multiply_one(half, final, c)
    for half in range(2):
        columns = pl.ds(half * COLS, COLS)
        wait(rights[half].at[other, final], core_recv.at[half, final])
        total = integrals[:, columns] + lax.dot_general(
            left_all[other, final], rights[half][other, final], (((0,), (0,)), ((), ())), preferred_element_type=F32
        )
        amplitude[:, columns] = (total * inverse[:, columns]).astype(BF16)

    def order(step):
        spot = step * 0
        for index, entry in enumerate(ORDER):
            spot = jnp.where(step == index, entry, spot)
        return spot

    def partial_rows(owner, dz):
        start = owner * PIECE + RANK[dz] * ROWS
        return slice(start, start + ROWS)

    def multiply_back(spot):
        total = None
        for half in range(2):
            term = lax.dot_general(
                rights[half][:, spot].reshape(2 * PIECE, COLS),
                amplitude[:, half * COLS : (half + 1) * COLS],
                (((1,), (1,)), ((), ())),
                preferred_element_type=F32,
            )
            total = term if total is None else total + term
        partial[spot] = total
        for way, dz in ((0, 1), (1, -1)):
            to = device_of(y, x, z + dz, c)
            opposite[spot, way] = total[partial_rows(way, 2)].astype(BF16)
            remote(opposite.at[spot, way], relay.at[spot, way], opposite_send, relay_recv.at[spot], to)
            straight = 1 - way
            ring_out[spot, way, straight] = total[partial_rows(straight, dz % RING)].astype(BF16)
            remote(
                ring_out.at[spot, way, straight], ring_in.at[spot, way, straight], ring_send, ring_recv.at[spot], to
            )

    def pass_on(spot):
        wait(relay.at[spot], relay_recv.at[spot])
        for way, dz in ((0, 1), (1, -1)):
            total = partial[spot, partial_rows(way, dz % RING), :] + relay[spot, way].astype(F32)
            ring_out[spot, way, way] = total.astype(BF16)
            remote(
                ring_out.at[spot, way, way], ring_in.at[spot, way, way], ring_send, ring_recv.at[spot],
                device_of(y, x, z + dz, c),
            )

    own_columns = pl.ds(pl.multiple_of((own_block % 8) * LEFT + c * LEFT_CORE, LEFT_CORE), LEFT_CORE)
    own_target = gamma.at[own_block // 8, :, own_columns]

    def hand_over(spot):
        wait(ring_in.at[spot], ring_recv.at[spot])
        for owner in range(2):
            total_out[2 * spot + owner] = (
                partial[spot, partial_rows(owner, 0), :]
                + ring_in[spot, 0, owner].astype(F32)
                + ring_in[spot, 1, owner].astype(F32)
            )

    def back(step, carry):
        @pl.when(step < PLANE)
        def _():
            multiply_back(order(step))

        @pl.when((step >= RELAY_LAG) & (step < PLANE + RELAY_LAG))
        def _():
            pass_on(order(step - RELAY_LAG))

        @pl.when(step >= RELAY_LAG + RING_LAG)
        def _():
            spot = order(step - RELAY_LAG - RING_LAG)
            hand_over(spot)

            @pl.when(step < PLANE + RELAY_LAG + RING_LAG - 1)
            def _():
                for owner in range(2):
                    remote(
                        total_out.at[2 * spot + owner], own_target, total_send, gamma_recv,
                        device_of(y + spot // RING, x + spot % RING, z, owner),
                    )

        return carry

    lax.fori_loop(0, PLANE + RELAY_LAG + RING_LAG, back, 0)
    remote(total_out.at[other], own_target, total_send, gamma_recv, sibling)
    keep = pltpu.make_async_copy(total_out.at[c], own_target, held_sem)
    keep.start()
    keep.wait()
    for sem in (gamma_recv, total_send):
        wait(total_out.at[pl.ds(0, 2 * PLANE - 1)], sem)

    wait(left.at[pl.ds(0, PLANE - 1), rows_of(0)], left_send)
    wait(left.at[:, pl.ds(0, PIECE - ROWS)], spread_send)
    wait(left_all.at[c], core_left.at[0])
    for half in range(2):
        wait(rights[half].at[c, 0, pl.ds(0, PIECE - ROWS)], right_send.at[half])
        wait(rights[half].at[c, pl.ds(0, PLANE - 1)], right_send.at[half])
        wait(rights[half].at[c], core_send.at[half])
    wait(opposite, opposite_send)
    wait(ring_out, ring_send)


def copy_kernel(source, target, held, sem):
    parts = [(n, pl.ds(row, 16), row // 16) for n in range(2) for row in range(0, ROWS, 16)]
    reads = [pltpu.make_async_copy(source.at[n, rows], held.at[n, rows], sem.at[0, n, k]) for n, rows, k in parts]
    writes = [pltpu.make_async_copy(held.at[n, rows], target.at[n, rows], sem.at[1, n, k]) for n, rows, k in parts]
    for read in reads:
        read.start()
    for read, write in zip(reads, writes):
        read.wait()
        write.start()
    for write in writes:
        write.wait()


def per_device(slabs, occ_energy, vir_energy, i_index, j_index):
    anywhere = pl.BlockSpec(memory_space=pl.ANY)
    dma = pltpu.SemaphoreType.DMA
    gamma = pl.pallas_call(
        kernel,
        out_shape=jax.ShapeDtypeStruct((2, ROWS, NVIR), F32),
        in_specs=[anywhere] * 5,
        out_specs=anywhere,
        scratch_shapes=[
            pltpu.VMEM((8, ROWS, NVIR), BF16),
            pltpu.VMEM((1, NVIR), jnp.int32),
            pltpu.SMEM((8,), jnp.int32),
            pltpu.SMEM((2,), jnp.int32),
            pltpu.SMEM((2,), jnp.int32),
            pltpu.VMEM((2, ROWS, NVIR), BF16),
            pltpu.VMEM((2, ROWS, NVIR), BF16),
            pltpu.VMEM((PLANE, PIECE, LEFT), BF16),
            pltpu.VMEM((2, PLANE, PIECE, LEFT_CORE), BF16),
            pltpu.VMEM((2, PLANE, PIECE, COLS), BF16),
            pltpu.VMEM((2, PLANE, PIECE, COLS), BF16),
            pltpu.VMEM((LEFT_CORE, RIGHT), F32),
            pltpu.VMEM((LEFT_CORE, RIGHT), BF16),
            pltpu.VMEM((LEFT_CORE, 128), F32),
            pltpu.VMEM((LEFT_CORE, RIGHT), F32),
            pltpu.VMEM((PLANE, 2 * PIECE, LEFT_CORE), F32),
            pltpu.VMEM((PLANE, 2, ROWS, LEFT_CORE), BF16),
            pltpu.VMEM((PLANE, 2, ROWS, LEFT_CORE), BF16),
            pltpu.VMEM((PLANE, 2, 2, ROWS, LEFT_CORE), BF16),
            pltpu.VMEM((PLANE, 2, 2, ROWS, LEFT_CORE), BF16),
            pltpu.VMEM((2 * PLANE, ROWS, LEFT_CORE), F32),
            dma, dma((5,)), dma, dma, dma, dma((RING,)), dma((3,)), dma((2,)), dma((2, 2)), dma((2, PLANE, 2)),
            dma((2,)), dma((2, PLANE)), dma, dma((PLANE,)), dma, dma((PLANE,)), dma, dma,
        ],
        compiler_params=pltpu.CompilerParams(
            collective_id=0, has_side_effects=True, vmem_limit_bytes=60 * 2**20
        ),
        name="back_transform",
    )(slabs, vir_energy.reshape(1, NVIR), occ_energy, i_index, j_index)
    return pl.pallas_call(
        copy_kernel,
        out_shape=jax.ShapeDtypeStruct((2, ROWS, NVIR), F32),
        in_specs=[anywhere],
        out_specs=anywhere,
        scratch_shapes=[pltpu.VMEM((2, ROWS, NVIR), F32), dma((2, 2, ROWS // 16))],
        name="result",
    )(gamma)


def solution(mesh):
    placed = (P(None, ("aux", "pan"), None), P(), P(), P(), P())
    return jax.shard_map(
        per_device,
        mesh=mesh,
        in_specs=placed,
        out_specs=P(None, ("aux", "pan"), None),
        check_vma=False,
    )
```
